32 devices in a mesh: sx: 4 (over z), sy: 8 (over y, x, core).
Axes of the slice: x: 2, y: 2, z: 4, core: 2. Of those that a mesh axis runs over, the one named last changes fastest.
Arguments:
- right_side: float32 [128, 128, 128], P('sx', 'sy'), may hold values from -48 to 48
- class_map: int32 [64, 64, 32], P('sx', 'sy'), may hold values from 0 to 7
- conductivity_table: float32 [8], replicated, may hold values from 0.2 to 5
- velocity: float32 [3, 128, 128, 128], P(None, 'sx', 'sy'), may hold values from -6 to 6
Outputs:
- potential: float32 [128, 128, 128], P('sx', 'sy')
- velocity_next: float32 [3, 128, 128, 128], P(None, ('sx', 'sy'))
The draws below stay inside these ranges and needn't reach their ends.
All inputs are finite; a program needn't handle non-finite values.
Results may differ from the reference program's by a relative error of at most 0.0003.
Values sent between devices are 32-bit elements; how exact they have to be, the bound alone decides.
A program may use at most 64 MiB of HBM per device.

```python
import math
import jax
import jax.numpy as jnp
from jax import lax

CX = 32
CY = 16
NZ = 128
MARGIN = 4
SWEEPS = 5
CLASSES = 8
NX = 128
NY = 128
N_SX = 4
N_SY = 8


def draw_right_side(key, part):
    cells_x = (jnp.arange(NX).astype(jnp.float32) + 0.5)[:, None, None] / NX
    cells_y = (jnp.arange(NY).astype(jnp.float32) + 0.5)[None, :, None] / NY
    random_part = jnp.clip(jax.random.normal(key, (NX, NY, NZ), jnp.float32), -4.0, 4.0)
    rising = jnp.exp(math.log(3.0) * (cells_x + cells_y))
    return random_part * rising


def plant(values, own_key, low, largest):
    longest = values.shape.index(max(values.shape))
    spots = []
    for shift in (0, 1):
        where = [jax.random.randint(jax.random.fold_in(own_key, axis), (), 0, length) for axis, length in enumerate(values.shape)]
        where[longest] = (where[longest] + shift) % values.shape[longest]
        spots.append(tuple(where))
    return values.at[spots[0]].set(low).at[spots[1]].set(largest)


def block_levels(rng, dims, cuts, smallest, high):
    def one(axis_at, shards_of):
        steps = jax.random.uniform(jax.random.fold_in(jax.random.fold_in(rng, 6), axis_at), (shards_of,), jnp.float32, smallest / len(cuts), high / len(cuts))
        return jnp.repeat(jnp.exp(steps), dims[axis_at] // shards_of).reshape((-1,) + (1,) * (len(dims) - axis_at - 1))

    loudness = one(*cuts[0])
    for cut in cuts[1:]:
        loudness = loudness * one(*cut)
    return loudness


def normal_values(own_key, dims, deviation, reach, pieces=(), kind=jnp.bfloat16):
    values = deviation * jax.random.normal(own_key, dims, jnp.float32)
    if pieces:
        values = values * block_levels(own_key, dims, pieces, -0.22, 0.18)
    return jnp.clip(values, -reach, reach).astype(kind)


def setup_inputs(seed: int = 0) -> dict:
    seeds = jax.random.split(jax.random.key(seed), 5)
    return {
        "right_side": draw_right_side(jax.random.fold_in(seeds[4], 71), 0),
        "class_map": plant(jax.random.randint(seeds[1], (NX // 2, NY // 2, NZ // 4), 0, CLASSES), jax.random.fold_in(seeds[1], 1), 0, CLASSES - 1).astype(jnp.int32),
        "conductivity_table": jnp.clip(jnp.exp(jax.random.uniform(seeds[2], (CLASSES,), jnp.float32, math.log(0.2), math.log(5.0))), 0.2, 5.0),
        "velocity": normal_values(seeds[3], (3, NX, NY, NZ), 1.0, 6.0, ((1, 4), (2, 8)), jnp.float32),
    }


axial_ratio = 0.0625
coupling = 0.25

def spatial_pad(grid_field):
    leading = [(0, 0)] * (grid_field.ndim - 3)
    return jnp.pad(grid_field, leading + [(1, 1), (1, 1), (1, 1)])

def coefficients(cond_padded):
    centre = cond_padded[..., 1:-1, 1:-1, 1:-1]
    face_terms = (0.5 * (centre + cond_padded[..., 2:, 1:-1, 1:-1]), 0.5 * (centre + cond_padded[..., :-2, 1:-1, 1:-1]), 0.5 * (centre + cond_padded[..., 1:-1, 2:, 1:-1]), 0.5 * (centre + cond_padded[..., 1:-1, :-2, 1:-1]), axial_ratio * 0.5 * (centre + cond_padded[..., 1:-1, 1:-1, 2:]), axial_ratio * 0.5 * (centre + cond_padded[..., 1:-1, 1:-1, :-2]))
    diagonal = face_terms[0] + face_terms[1] + face_terms[2] + face_terms[3] + face_terms[4] + face_terms[5]
    return (face_terms, diagonal)

def apply_operator(face_terms, diagonal, padded):
    centre = padded[..., 1:-1, 1:-1, 1:-1]
    beside = face_terms[0] * padded[..., 2:, 1:-1, 1:-1] + face_terms[1] * padded[..., :-2, 1:-1, 1:-1]
    beside = beside + face_terms[2] * padded[..., 1:-1, 2:, 1:-1] + face_terms[3] * padded[..., 1:-1, :-2, 1:-1]
    beside = beside + face_terms[4] * padded[..., 1:-1, 1:-1, 2:] + face_terms[5] * padded[..., 1:-1, 1:-1, :-2]
    return diagonal * centre - beside

def local_sweeps(cond_region, residual_region):
    face_terms, diagonal = coefficients(spatial_pad(cond_region))
    inside = (cond_region > 0.0).astype(jnp.float32)
    inverse = inside / (diagonal + (1.0 - inside))
    update = residual_region * inverse
    for sweep_index in range(SWEEPS - 1):
        update = update + (residual_region - apply_operator(face_terms, diagonal, spatial_pad(update))) * inverse
    return update

def schwarz(conductivity, residual):
    pads = ((MARGIN, MARGIN), (MARGIN, MARGIN), (0, 0))
    wide_cond = jnp.pad(conductivity, pads)
    wide_res = jnp.pad(residual, pads)
    columns = jnp.arange(N_SY, dtype=jnp.int32)[:, None] * CY + jnp.arange(CY + 2 * MARGIN, dtype=jnp.int32)[None, :]

    def one_row(block_index):
        row_start = (block_index * CX).astype(jnp.int32)
        rows_cond = lax.dynamic_slice_in_dim(wide_cond, row_start, CX + 2 * MARGIN, 0)
        rows_res = lax.dynamic_slice_in_dim(wide_res, row_start, CX + 2 * MARGIN, 0)
        region_cond = jnp.moveaxis(rows_cond[:, columns, :], 1, 0)
        region_res = jnp.moveaxis(rows_res[:, columns, :], 1, 0)
        update = local_sweeps(region_cond, region_res)
        own_cells = update[:, MARGIN:MARGIN + CX, MARGIN:MARGIN + CY, :]
        return jnp.moveaxis(own_cells, 0, 1).reshape(CX, NY, NZ)
    blocks = lax.map(one_row, jnp.arange(N_SX, dtype=jnp.int32))
    return blocks.reshape(NX, NY, NZ)

def sine_table(lines_count):
    positions = jnp.arange(lines_count, dtype=jnp.int32) + 1
    phase_index = positions[:, None] * positions[None, :] % (2 * (lines_count + 1))
    return jnp.sqrt(2.0 / (lines_count + 1)) * jnp.sin(jnp.pi * phase_index.astype(jnp.float32) / (lines_count + 1))

def diffusion_gain(lines_count, cells_side):
    positions = (jnp.arange(lines_count, dtype=jnp.int32) + 1).astype(jnp.float32)
    half_sine = jnp.sin(0.5 * jnp.pi * positions / (lines_count + 1))
    stiffness = 8.0 * cells_side * cells_side * half_sine * half_sine
    return (1.0 - stiffness) / (1.0 + stiffness)

def reference(right_side, class_map, conductivity_table, velocity):
    block_values = conductivity_table[class_map]
    conductivity = jnp.repeat(jnp.repeat(jnp.repeat(block_values, 2, axis=0), 2, axis=1), 4, axis=2)
    own_faces, own_diagonal = coefficients(spatial_pad(conductivity))

    def operate(grid_field):
        return apply_operator(own_faces, own_diagonal, spatial_pad(grid_field))
    residual = right_side
    first_dir = schwarz(conductivity, residual)
    image_one = operate(first_dir)
    weight_one = jnp.sum(image_one * image_one)
    alpha_one = jnp.sum(residual * image_one) / weight_one
    residual = residual - alpha_one * image_one
    second_dir = schwarz(conductivity, residual)
    image_two = operate(second_dir)
    beta_two = jnp.sum(image_two * image_one) / weight_one
    image_two = image_two - beta_two * image_one
    second_dir = second_dir - beta_two * first_dir
    alpha_two = jnp.sum(residual * image_two) / jnp.sum(image_two * image_two)
    potential = alpha_one * first_dir
    potential = potential + alpha_two * second_dir
    padded = spatial_pad(potential)
    grad_x = 0.5 * (padded[2:, 1:-1, 1:-1] - padded[:-2, 1:-1, 1:-1])
    grad_y = 0.5 * (padded[1:-1, 2:, 1:-1] - padded[1:-1, :-2, 1:-1])
    force_x = conductivity * (-grad_y - velocity[0])
    force_y = conductivity * (grad_x - velocity[1])
    moved_velocity = jnp.stack([velocity[0] + coupling * force_x, velocity[1] + coupling * force_y, velocity[2]])
    sine_rows = sine_table(NY)
    line_gain = diffusion_gain(NY, CY)[:, None]
    sine_coeffs = jnp.matmul(sine_rows, moved_velocity, precision=lax.Precision.HIGHEST)
    velocity_next = jnp.matmul(sine_rows, sine_coeffs * line_gain, precision=lax.Precision.HIGHEST)
    return (potential, velocity_next)
```

```python
import functools

import jax
import jax.numpy as jnp
import numpy as np
from jax import lax
from jax.experimental import pallas as pl
from jax.experimental.pallas import tpu as pltpu
from jax.sharding import PartitionSpec as P

MARGIN = 4
SWEEPS = 5
CLASSES = 8

axial_ratio = 0.0625
coupling = 0.25
highest = lax.Precision.HIGHEST
MESH = pl.DeviceIdType.MESH
DIAGONALS = ((-1, -1), (-1, 1), (1, -1), (1, 1))


def line_matrix(lines_count, cells_side):
    positions = np.arange(lines_count, dtype=np.int64) + 1
    phase = (positions[:, None] * positions[None, :]) % (2 * (lines_count + 1))
    sines = np.sqrt(2.0 / (lines_count + 1)) * np.sin(np.pi * phase / (lines_count + 1))
    half = np.sin(0.5 * np.pi * positions / (lines_count + 1))
    stiff = 8.0 * cells_side * cells_side * half * half
    gain = (1.0 - stiff) / (1.0 + stiff)
    return ((sines * gain[None, :]) @ sines).astype(np.float32)


def kernel(
    n_sx, n_sy, right_ref, class_ref, table_ref, velocity_ref, matrix_ref,
    potential_ref, next_ref,
    blk, blk_y, blk_c, got_bx, got_by, got_bc, wide_blk, cond,
    res_y, res_c, got_rx, got_ry, got_rc,
    img_y, img_c, got_ix, got_iy, got_ic,
    first_y, got_fx, got_fy, q_y, got_qx, got_qy,
    region, start, buf_a, buf_b, buf_q,
    bxp, bxm, byp, bym, bzp, bzm, inv, diag,
    first_own, image, q_own,
    line_v, line_c, line_f, line_q, sums_mine, sums_x, sums_row, sums_y,
    halo_send, halo_recv, face_send, face_recv, a2a_send, a2a_recv, local_sem,
    sx_send, sx_recv, sy_send, sy_recv,
):
    p, q = lax.axis_index("sx"), lax.axis_index("sy")
    cx, cy, nz = right_ref.shape
    hx, hy = cx // 2, cy // 2
    m = cx // n_sy
    mb = max(1, m // 2)
    ex, ey = cx + 2 * MARGIN, cy + 2 * MARGIN
    M = MARGIN
    H = M // 2
    lines_count = cy * n_sy

    def exists(dx, dy):
        ok = None
        for at, d, n in ((p, dx, n_sx), (q, dy, n_sy)):
            if d:
                this = (at + d >= 0) & (at + d < n)
                ok = this if ok is None else ok & this
        return ok

    barrier = pltpu.get_barrier_semaphore()

    def greet_y(k, _):
        pl.semaphore_signal(barrier, inc=1, device_id=(p, lax.rem(q + k, n_sy)), device_id_type=MESH)
        return 0

    def greet_x(k, _):
        pl.semaphore_signal(barrier, inc=1, device_id=(lax.rem(p + k, n_sx), q), device_id_type=MESH)
        return 0

    lax.fori_loop(1, n_sy, greet_y, 0)
    lax.fori_loop(1, n_sx, greet_x, 0)
    for dx, dy in DIAGONALS:
        @pl.when(exists(dx, dy))
        def _(dx=dx, dy=dy):
            pl.semaphore_signal(barrier, inc=1, device_id=(p + dx, q + dy), device_id_type=MESH)

    classes = class_ref[...].reshape(hx * hy, class_ref.shape[2])
    picked = jnp.zeros(classes.shape, jnp.float32)
    for one in range(CLASSES):
        picked = jnp.where(classes == one, table_ref[one], picked)
    zb = classes.shape[1]
    per = nz // zb
    wide = lax.broadcasted_iota(jnp.int32, (zb, nz), 1) - per * lax.broadcasted_iota(jnp.int32, (zb, nz), 0)
    spread = jnp.where((wide >= 0) & (wide < per), 1.0, 0.0).astype(jnp.float32)
    blk[...] = jnp.dot(picked, spread, precision=highest, preferred_element_type=jnp.float32).reshape(hx, hy, nz)
    blk_y[0] = blk[:, 0:H, :]
    blk_y[1] = blk[:, hy - H : hy, :]
    res_y[0] = right_ref[:, 0:M, :]
    res_y[1] = right_ref[:, cy - M : cy, :]
    for at, (dx, dy) in enumerate(DIAGONALS):
        bx0, by0 = (0 if dx < 0 else hx - H), (0 if dy < 0 else hy - H)
        rx0, ry0 = (0 if dx < 0 else cx - M), (0 if dy < 0 else cy - M)
        blk_c[at] = blk[bx0 : bx0 + H, by0 : by0 + H, :]
        res_c[at] = right_ref[rx0 : rx0 + M, ry0 : ry0 + M, :]

    for at, (dx, dy) in enumerate(((-1, 0), (1, 0))):
        @pl.when(jnp.logical_not(exists(dx, dy)))
        def _(at=at):
            for ref in (got_bx, got_rx, got_ix, got_fx, got_qx):
                ref[at] = jnp.zeros(ref.shape[1:], jnp.float32)

    for at, (dx, dy) in enumerate(((0, -1), (0, 1))):
        @pl.when(jnp.logical_not(exists(dx, dy)))
        def _(at=at):
            for ref in (got_by, got_ry, got_iy, got_fy, got_qy):
                ref[at] = jnp.zeros(ref.shape[1:], jnp.float32)

    for at, (dx, dy) in enumerate(DIAGONALS):
        @pl.when(jnp.logical_not(exists(dx, dy)))
        def _(at=at):
            for ref in (got_bc, got_rc, got_ic):
                ref[at] = jnp.zeros(ref.shape[1:], jnp.float32)

    diagonal_count = sum(jnp.where(exists(dx, dy), 1, 0) for dx, dy in DIAGONALS)
    pl.semaphore_wait(barrier, n_sy - 1 + n_sx - 1 + diagonal_count)

    def exchange(number, x_parts, y_parts, c_parts, got_x, got_y, got_c):
        routes = []
        for at, (dx, dy) in enumerate(((-1, 0), (1, 0))):
            routes.append((dx, dy, x_parts[at], got_x.at[1 - at], got_x.at[at], at))
        for at, (dx, dy) in enumerate(((0, -1), (0, 1))):
            routes.append((dx, dy, y_parts[at], got_y.at[1 - at], got_y.at[at], 2 + at))
        if got_c is not None:
            for at, (dx, dy) in enumerate(DIAGONALS):
                routes.append((dx, dy, c_parts[at], got_c.at[3 - at], got_c.at[at], 4 + at))
        send, recv = (halo_send, halo_recv) if got_c is not None else (face_send, face_recv)
        opposite = (1, 0, 3, 2, 7, 6, 5, 4)

        def copy(dx, dy, src, dst, slot):
            return pltpu.make_async_remote_copy(
                src_ref=src, dst_ref=dst, send_sem=send.at[number, slot],
                recv_sem=recv.at[number, opposite[slot]],
                device_id=(p + dx, q + dy), device_id_type=MESH,
            )

        for dx, dy, src, dst, mine, slot in routes:
            @pl.when(exists(dx, dy))
            def _(dx=dx, dy=dy, src=src, dst=dst, slot=slot):
                copy(dx, dy, src, dst, slot).start()

        def arrive():
            for dx, dy, src, dst, mine, slot in routes:
                @pl.when(exists(dx, dy))
                def _(dx=dx, dy=dy, src=src, mine=mine, slot=slot):
                    pltpu.make_async_remote_copy(
                        src_ref=src, dst_ref=mine, send_sem=send.at[number, slot],
                        recv_sem=recv.at[number, slot],
                        device_id=(p + dx, q + dy), device_id_type=MESH,
                    ).wait_recv()

        def leave():
            for dx, dy, src, dst, mine, slot in routes:
                @pl.when(exists(dx, dy))
                def _(dx=dx, dy=dy, src=src, dst=dst, slot=slot):
                    copy(dx, dy, src, dst, slot).wait_send()

        return arrive, leave

    def to_lines(number, source, target):
        def rows(who):
            return pl.ds(pl.multiple_of(who * cy, cy), cy)

        def copy(other, sender):
            return pltpu.make_async_remote_copy(
                src_ref=source(other), dst_ref=target(sender), send_sem=a2a_send.at[number, other],
                recv_sem=a2a_recv.at[number, sender], device_id=(p, other), device_id_type=MESH,
            )

        def begin(k, _):
            copy(lax.rem(q + k, n_sy), q).start()
            return 0

        def finish(k, _):
            other = lax.rem(q + k, n_sy)
            copy(other, q).wait_send()
            copy(other, other).wait_recv()
            return 0

        lax.fori_loop(1, n_sy, begin, 0)
        own = pltpu.make_async_copy(source(q), target(q), local_sem.at[number])
        own.start()

        def complete():
            lax.fori_loop(1, n_sy, finish, 0)
            own.wait()

        return complete

    def lines(who):
        return pl.ds(pl.multiple_of(who * cy, cy), cy)

    def half_lines(who):
        return pl.ds(pl.multiple_of(who * hy, hy), hy)

    blk_arrive, blk_leave = exchange(
        0, (blk.at[pl.ds(0, H)], blk.at[pl.ds(hx - H, H)]), (blk_y.at[0], blk_y.at[1]),
        [blk_c.at[at] for at in range(4)], got_bx, got_by, got_bc)
    res_arrive, res_leave = exchange(
        1, (right_ref.at[pl.ds(0, M)], right_ref.at[pl.ds(cx - M, M)]), (res_y.at[0], res_y.at[1]),
        [res_c.at[at] for at in range(4)], got_rx, got_ry, got_rc)
    lines_c = to_lines(
        0, lambda s: blk.at[pl.ds((s * m) // 2, mb)], lambda s: line_c.at[:, half_lines(s), :])
    lines_v = to_lines(
        1, lambda s: velocity_ref.at[:, pl.ds(s * m, m)], lambda s: line_v.at[:, :, lines(s), :])

    blk_arrive()
    wide_blk[H : H + hx, H : H + hy, :] = blk[...]
    wide_blk[0:H, H : H + hy, :] = got_bx[0]
    wide_blk[H + hx : hx + 2 * H, H : H + hy, :] = got_bx[1]
    wide_blk[H : H + hx, 0:H, :] = got_by[0]
    wide_blk[H : H + hx, H + hy : hy + 2 * H, :] = got_by[1]
    for at, (dx, dy) in enumerate(DIAGONALS):
        x0, y0 = (0 if dx < 0 else H + hx), (0 if dy < 0 else H + hy)
        wide_blk[x0 : x0 + H, y0 : y0 + H, :] = got_bc[at]
    cond[0] = jnp.zeros((ey, nz), jnp.float32)
    cond[ex // 2 + 1] = jnp.zeros((ey, nz), jnp.float32)
    for j in range(ey // 2):
        cond[1 : ex // 2 + 1, 2 * j : 2 * j + 2, :] = jnp.broadcast_to(
            wide_blk[:, j : j + 1, :], (ex // 2, 2, nz))

    row_at = lax.broadcasted_iota(jnp.int32, (ey, nz), 0)
    lane_at = lax.broadcasted_iota(jnp.int32, (ey, nz), 1)

    def coefficients(pair, _):
        before, here, after = cond[pair], cond[pair + 1], cond[pair + 2]
        yp = jnp.where(row_at < ey - 1, pltpu.roll(here, ey - 1, 0), 0.0)
        ym = jnp.where(row_at > 0, pltpu.roll(here, 1, 0), 0.0)
        zp = jnp.where(lane_at < nz - 1, pltpu.roll(here, nz - 1, 1), 0.0)
        zm = jnp.where(lane_at > 0, pltpu.roll(here, 1, 1), 0.0)
        ayp, aym = 0.5 * (here + yp), 0.5 * (here + ym)
        azp, azm = (axial_ratio * 0.5) * (here + zp), (axial_ratio * 0.5) * (here + zm)
        across = ayp + aym + azp + azm
        azp = jnp.where(lane_at < nz - 1, azp, 0.0)
        azm = jnp.where(lane_at > 0, azm, 0.0)
        for side, (xp, xm) in enumerate(((here, before), (after, here))):
            x = 2 * pair + side
            axp, axm = 0.5 * (here + xp), 0.5 * (here + xm)
            total = axp + axm + across
            inside = here > 0.0
            over = jnp.where(inside, 1.0 / jnp.where(inside, total, 1.0), 0.0)
            diag[x] = total
            inv[x] = over
            bxp[x] = axp * over
            bxm[x] = axm * over
            byp[x] = ayp * over
            bym[x] = aym * over
            bzp[x] = azp * over
            bzm[x] = azm * over
        return 0

    lax.fori_loop(0, ex // 2, coefficients, 0)

    def assemble(own, got_x, got_y, got_c):
        region[M : M + cx, M : M + cy, :] = own[...]
        region[0:M, M : M + cy, :] = got_x[0]
        region[M + cx : ex, M : M + cy, :] = got_x[1]
        region[M : M + cx, 0:M, :] = got_y[0]
        region[M : M + cx, M + cy : ey, :] = got_y[1]
        for at, (dx, dy) in enumerate(DIAGONALS):
            x0, y0 = (0 if dx < 0 else M + cx), (0 if dy < 0 else M + cy)
            region[x0 : x0 + M, y0 : y0 + M, :] = got_c[at]

    def beside(x, below, centre, above):
        total = bxp[x] * above + bxm[x] * below
        total = total + byp[x] * pltpu.roll(centre, ey - 1, 0) + bym[x] * pltpu.roll(centre, 1, 0)
        return total + bzp[x] * pltpu.roll(centre, nz - 1, 1) + bzm[x] * pltpu.roll(centre, 1, 1)

    def precondition(target):
        def begin(pair, _):
            for x in (2 * pair, 2 * pair + 1):
                start[x] = region[x] * inv[x]
            return 0

        lax.fori_loop(0, ex // 2, begin, 0)
        src = start
        for sweep in range(1, SWEEPS):
            dst = target if sweep == SWEEPS - 1 else (buf_a if sweep % 2 else buf_b)

            def body(pair, _, src=src, dst=dst, sweep=sweep):
                x = sweep + 2 * pair
                rows = [src[x - 1 + i] for i in range(4)]
                for i in range(2):
                    dst[x + i] = start[x + i] + beside(x + i, rows[i], rows[i + 1], rows[i + 2])
                return 0

            lax.fori_loop(0, (ex - 2 * sweep) // 2, body, 0)
            src = dst

    def send_faces(number, field, packed, got_x, got_y):
        packed[0] = field[M : M + cx, M : M + 1, :]
        packed[1] = field[M : M + cx, M + cy - 1 : M + cy, :]
        return exchange(
            number, (field.at[M], field.at[M + cx - 1]), (packed.at[0], packed.at[1]), None, got_x, got_y, None)

    def place_faces(field, own, got_x, got_y):
        field[M - 1] = got_x[0]
        field[M + cx] = got_x[1]
        field[M : M + cx, M - 1 : M, :] = got_y[0]
        field[M : M + cx, M + cy : M + cy + 1, :] = got_y[1]
        own[...] = field[M - 1 : M + cx + 1, M : M + cy, :]

    def operate(field, x):
        centre = field[x]
        return (diag[x] * (centre - beside(x, field[x - 1], centre, field[x + 1])))[M : M + cy, :]

    res_arrive()
    assemble(right_ref, got_rx, got_ry, got_rc)
    precondition(buf_b)
    face_arrive, face_leave = send_faces(0, buf_b, first_y, got_fx, got_fy)
    face_arrive()
    face_leave()
    place_faces(buf_b, first_own, got_fx, got_fy)

    def first_image(pair, _):
        for i in range(2):
            x = 2 * pair + i
            image[x] = operate(buf_b, M + x)
        return 0

    lax.fori_loop(0, cx // 2, first_image, 0)
    img_y[0] = image[:, 0:M, :]
    img_y[1] = image[:, cy - M : cy, :]
    for at, (dx, dy) in enumerate(DIAGONALS):
        x0, y0 = (0 if dx < 0 else cx - M), (0 if dy < 0 else cy - M)
        img_c[at] = image[x0 : x0 + M, y0 : y0 + M, :]
    img_arrive, img_leave = exchange(
        2, (image.at[pl.ds(0, M)], image.at[pl.ds(cx - M, M)]), (img_y.at[0], img_y.at[1]),
        [img_c.at[at] for at in range(4)], got_ix, got_iy, got_ic)
    lines_f = to_lines(
        2, lambda s: first_own.at[pl.ds(s * m, m + 2)], lambda s: line_f.at[:, lines(s), :])

    img_arrive()
    assemble(image, got_ix, got_iy, got_ic)
    precondition(buf_q)
    q_arrive, q_leave = send_faces(1, buf_q, q_y, got_qx, got_qy)
    q_arrive()
    q_leave()
    place_faces(buf_q, q_own, got_qx, got_qy)
    lines_q = to_lines(
        3, lambda s: q_own.at[pl.ds(s * m, m + 2)], lambda s: line_q.at[:, lines(s), :])

    def products(x, carry):
        ri, ii, wi, ww, rw = carry
        r, i, w = right_ref[x], image[x], operate(buf_q, M + x)
        return ri + r * i, ii + i * i, wi + w * i, ww + w * w, rw + r * w

    zero = jnp.zeros((cy, nz), jnp.float32)
    totals = lax.fori_loop(0, cx, products, (zero,) * 5)
    packed = jnp.zeros((8, nz), jnp.float32)
    row8 = lax.broadcasted_iota(jnp.int32, (8, nz), 0)
    for at, total in enumerate(totals):
        packed = jnp.where(row8 == at, jnp.sum(total, axis=0, keepdims=True), packed)
    sums_mine[...] = packed

    def gather(axis_at, count, mine, slots, send, recv, device):
        def copy(other, sender):
            return pltpu.make_async_remote_copy(
                src_ref=mine, dst_ref=slots.at[sender], send_sem=send.at[other],
                recv_sem=recv.at[sender], device_id=device(other), device_id_type=MESH)

        def begin(k, _):
            copy(lax.rem(axis_at + k, count), axis_at).start()
            return 0

        def finish(k, _):
            other = lax.rem(axis_at + k, count)
            copy(other, axis_at).wait_send()
            copy(other, other).wait_recv()
            return 0

        lax.fori_loop(1, count, begin, 0)
        slots[axis_at] = mine[...]

        def complete():
            lax.fori_loop(1, count, finish, 0)
            return jnp.sum(slots[...], axis=0)

        return complete

    row_sums = gather(p, n_sx, sums_mine, sums_x, sx_send, sx_recv, lambda other: (other, q))
    lines_v()
    lines_c()
    lines_f()
    matrix = matrix_ref[...]
    for row in range(m):
        next_ref[2, row] = jnp.dot(
            matrix, line_v[2, row], precision=highest, preferred_element_type=jnp.float32)
    sums_row[...] = row_sums()
    all_sums = gather(q, n_sy, sums_row, sums_y, sy_send, sy_recv, lambda other: (p, other))
    blk_leave()
    res_leave()
    img_leave()
    scalars = jnp.sum(all_sums(), axis=1, keepdims=True)
    ri, ii, wi, ww, rw = (scalars[at : at + 1, :] for at in range(5))
    alpha = ri / ii
    gamma = wi / ii
    kappa = (gamma * ri - rw) / (ww - gamma * wi)
    of_first = alpha + kappa * gamma

    def own_potential(x, _):
        potential_ref[x] = of_first * first_own[x + 1] - kappa * q_own[x + 1]
        return 0

    lax.fori_loop(0, cx, own_potential, 0)

    lines_q()
    line_at = lax.broadcasted_iota(jnp.int32, (lines_count, nz), 0)
    planes = [of_first * line_f[row] - kappa * line_q[row] for row in range(m + 2)]
    for row in range(m):
        here = planes[row + 1]
        grad_x = 0.5 * (planes[row + 2] - planes[row])
        up = jnp.where(line_at < lines_count - 1, pltpu.roll(here, lines_count - 1, 0), 0.0)
        down = jnp.where(line_at > 0, pltpu.roll(here, 1, 0), 0.0)
        grad_y = 0.5 * (up - down)
        compact = line_c[row // 2]
        c = coupling * jnp.broadcast_to(
            compact[:, None, :], (lines_count // 2, 2, nz)).reshape(lines_count, nz)
        vx, vy = line_v[0, row], line_v[1, row]
        next_ref[0, row] = jnp.dot(
            matrix, vx + c * (-grad_y - vx), precision=highest, preferred_element_type=jnp.float32)
        next_ref[1, row] = jnp.dot(
            matrix, vy + c * (grad_x - vy), precision=highest, preferred_element_type=jnp.float32)


def per_device(n_sx, n_sy, right_side, class_map, conductivity_table, velocity):
    cx, cy, nz = right_side.shape
    m = cx // n_sy
    assert m * n_sy == cx and (m == 1 or m % 2 == 0)
    mb = max(1, m // 2)
    hx, hy = cx // 2, cy // 2
    M, H = MARGIN, MARGIN // 2
    ex, ey = cx + 2 * M, cy + 2 * M
    ny = cy * n_sy
    matrix = jnp.asarray(line_matrix(ny, cy))

    def vmem(*shape):
        return pltpu.VMEM(shape, jnp.float32)

    wide = vmem(ex, ey, nz)
    whole = pl.BlockSpec(memory_space=pltpu.VMEM)
    dma = pltpu.SemaphoreType.DMA
    scratch = [
        vmem(hx, hy, nz), vmem(2, hx, H, nz), vmem(4, H, H, nz),
        vmem(2, H, hy, nz), vmem(2, hx, H, nz), vmem(4, H, H, nz),
        vmem(ex // 2, ey // 2, nz), vmem(ex // 2 + 2, ey, nz),
        vmem(2, cx, M, nz), vmem(4, M, M, nz),
        vmem(2, M, cy, nz), vmem(2, cx, M, nz), vmem(4, M, M, nz),
        vmem(2, cx, M, nz), vmem(4, M, M, nz),
        vmem(2, M, cy, nz), vmem(2, cx, M, nz), vmem(4, M, M, nz),
        vmem(2, cx, 1, nz), vmem(2, ey, nz), vmem(2, cx, 1, nz),
        vmem(2, cx, 1, nz), vmem(2, ey, nz), vmem(2, cx, 1, nz),
        wide, wide, wide, wide, wide,
        wide, wide, wide, wide, wide, wide, wide, wide,
        vmem(cx + 2, cy, nz), vmem(cx, cy, nz), vmem(cx + 2, cy, nz),
        vmem(3, m, ny, nz), vmem(mb, ny // 2, nz), vmem(m + 2, ny, nz), vmem(m + 2, ny, nz),
        vmem(8, nz), vmem(n_sx, 8, nz), vmem(8, nz), vmem(n_sy, 8, nz),
        dma((3, 8)), dma((3, 8)), dma((2, 8)), dma((2, 8)),
        dma((4, n_sy)), dma((4, n_sy)), dma((4,)),
        dma((n_sx,)), dma((n_sx,)), dma((n_sy,)), dma((n_sy,)),
    ]
    return pl.pallas_call(
        functools.partial(kernel, n_sx, n_sy),
        out_shape=(
            jax.ShapeDtypeStruct((cx, cy, nz), jnp.float32),
            jax.ShapeDtypeStruct((3, m, ny, nz), jnp.float32),
        ),
        in_specs=[
            whole, whole, pl.BlockSpec(memory_space=pltpu.SMEM),
            pl.BlockSpec(memory_space=pl.ANY), whole,
        ],
        out_specs=(whole, whole),
        scratch_shapes=scratch,
        compiler_params=pltpu.CompilerParams(
            collective_id=0, has_side_effects=True, vmem_limit_bytes=40 * 2**20),
    )(right_side, class_map, conductivity_table, velocity, matrix)


def solution(mesh):
    return jax.shard_map(
        functools.partial(per_device, mesh.shape["sx"], mesh.shape["sy"]),
        mesh=mesh,
        in_specs=(P("sx", "sy", None), P("sx", "sy", None), P(), P(None, "sx", "sy", None)),
        out_specs=(P("sx", "sy", None), P(None, ("sx", "sy"), None, None)),
        check_vma=False,
    )
```

```python
import functools

import jax
import jax.numpy as jnp
import numpy as np
from jax import lax
from jax.experimental import pallas as pl
from jax.experimental.pallas import tpu as pltpu
from jax.sharding import PartitionSpec as P

MARGIN = 4
SWEEPS = 5
CLASSES = 8

axial_ratio = 0.0625
coupling = 0.25
highest = lax.Precision.HIGHEST
MESH = pl.DeviceIdType.MESH
DIAGONALS = ((-1, -1), (-1, 1), (1, -1), (1, 1))


def line_matrix(lines_count, cells_side):
    positions = np.arange(lines_count, dtype=np.int64) + 1
    phase = (positions[:, None] * positions[None, :]) % (2 * (lines_count + 1))
    sines = np.sqrt(2.0 / (lines_count + 1)) * np.sin(np.pi * phase / (lines_count + 1))
    half = np.sin(0.5 * np.pi * positions / (lines_count + 1))
    stiff = 8.0 * cells_side * cells_side * half * half
    gain = (1.0 - stiff) / (1.0 + stiff)
    return ((sines * gain[None, :]) @ sines).astype(np.float32)


def kernel(
    n_sx, n_sy, right_hbm, class_hbm, table_hbm, velocity_ref, matrix_hbm,
    potential_hbm, next_hbm,
    potential_ref, next_ref, store_sem,
    right_ref, class_ref, table_ref, matrix_ref, load_sem,
    blk, blk_y, blk_c, got_bx, got_by, got_bc, wide_blk, cond,
    res_y, res_c, got_rx, got_ry, got_rc,
    img_y, img_c, got_ix, got_iy, got_ic,
    first_y, got_fx, got_fy, q_y, got_qx, got_qy,
    region, start, buf_a, buf_b, buf_q,
    bxp, bxm, byp, bym, bzp, bzm, inv, diag,
    first_own, image, q_own,
    line_v, line_c, line_f, line_q, sums_mine, sums_x, sums_row, sums_y,
    halo_send, halo_recv, face_send, face_recv, a2a_send, a2a_recv, local_sem,
    sx_send, sx_recv, sy_send, sy_recv,
):
    p, q = lax.axis_index("sx"), lax.axis_index("sy")
    cx, cy, nz = right_ref.shape
    hx, hy = cx // 2, cy // 2
    m = cx // n_sy
    mb = max(1, m // 2)
    ex, ey = cx + 2 * MARGIN, cy + 2 * MARGIN
    M = MARGIN
    H = M // 2
    lines_count = cy * n_sy

    def exists(dx, dy):
        ok = None
        for at, d, n in ((p, dx, n_sx), (q, dy, n_sy)):
            if d:
                this = (at + d >= 0) & (at + d < n)
                ok = this if ok is None else ok & this
        return ok

    loads = [
        pltpu.make_async_copy(src, dst, load_sem.at[at])
        for at, (src, dst) in enumerate((
            (class_hbm, class_ref), (table_hbm, table_ref), (right_hbm, right_ref), (matrix_hbm, matrix_ref)))
    ]
    for load in loads:
        load.start()

    barrier = pltpu.get_barrier_semaphore()

    def greet_y(k, _):
        pl.semaphore_signal(barrier, inc=1, device_id=(p, lax.rem(q + k, n_sy)), device_id_type=MESH)
        return 0

    def greet_x(k, _):
        pl.semaphore_signal(barrier, inc=1, device_id=(lax.rem(p + k, n_sx), q), device_id_type=MESH)
        return 0

    lax.fori_loop(1, n_sy, greet_y, 0)
    lax.fori_loop(1, n_sx, greet_x, 0)
    for dx, dy in DIAGONALS:
        @pl.when(exists(dx, dy))
        def _(dx=dx, dy=dy):
            pl.semaphore_signal(barrier, inc=1, device_id=(p + dx, q + dy), device_id_type=MESH)

    loads[0].wait()
    loads[1].wait()
    classes = class_ref[...].reshape(hx * hy, class_ref.shape[2])
    picked = jnp.zeros(classes.shape, jnp.float32)
    for one in range(CLASSES):
        picked = jnp.where(classes == one, table_ref[one], picked)
    zb = classes.shape[1]
    per = nz // zb
    wide = lax.broadcasted_iota(jnp.int32, (zb, nz), 1) - per * lax.broadcasted_iota(jnp.int32, (zb, nz), 0)
    spread = jnp.where((wide >= 0) & (wide < per), 1.0, 0.0).astype(jnp.float32)
    blk[...] = jnp.dot(picked, spread, precision=highest, preferred_element_type=jnp.float32).reshape(hx, hy, nz)
    blk_y[0] = blk[:, 0:H, :]
    blk_y[1] = blk[:, hy - H : hy, :]
    loads[2].wait()
    res_y[0] = right_ref[:, 0:M, :]
    res_y[1] = right_ref[:, cy - M : cy, :]
    for at, (dx, dy) in enumerate(DIAGONALS):
        bx0, by0 = (0 if dx < 0 else hx - H), (0 if dy < 0 else hy - H)
        rx0, ry0 = (0 if dx < 0 else cx - M), (0 if dy < 0 else cy - M)
        blk_c[at] = blk[bx0 : bx0 + H, by0 : by0 + H, :]
        res_c[at] = right_ref[rx0 : rx0 + M, ry0 : ry0 + M, :]

    for at, (dx, dy) in enumerate(((-1, 0), (1, 0))):
        @pl.when(jnp.logical_not(exists(dx, dy)))
        def _(at=at):
            for ref in (got_bx, got_rx, got_ix, got_fx, got_qx):
                ref[at] = jnp.zeros(ref.shape[1:], jnp.float32)

    for at, (dx, dy) in enumerate(((0, -1), (0, 1))):
        @pl.when(jnp.logical_not(exists(dx, dy)))
        def _(at=at):
            for ref in (got_by, got_ry, got_iy, got_fy, got_qy):
                ref[at] = jnp.zeros(ref.shape[1:], jnp.float32)

    for at, (dx, dy) in enumerate(DIAGONALS):
        @pl.when(jnp.logical_not(exists(dx, dy)))
        def _(at=at):
            for ref in (got_bc, got_rc, got_ic):
                ref[at] = jnp.zeros(ref.shape[1:], jnp.float32)

    diagonal_count = sum(jnp.where(exists(dx, dy), 1, 0) for dx, dy in DIAGONALS)
    pl.semaphore_wait(barrier, n_sy - 1 + n_sx - 1 + diagonal_count)

    def exchange(number, x_parts, y_parts, c_parts, got_x, got_y, got_c):
        routes = []
        for at, (dx, dy) in enumerate(((-1, 0), (1, 0))):
            routes.append((dx, dy, x_parts[at], got_x.at[1 - at], got_x.at[at], at))
        for at, (dx, dy) in enumerate(((0, -1), (0, 1))):
            routes.append((dx, dy, y_parts[at], got_y.at[1 - at], got_y.at[at], 2 + at))
        if got_c is not None:
            for at, (dx, dy) in enumerate(DIAGONALS):
                routes.append((dx, dy, c_parts[at], got_c.at[3 - at], got_c.at[at], 4 + at))
        send, recv = (halo_send, halo_recv) if got_c is not None else (face_send, face_recv)
        opposite = (1, 0, 3, 2, 7, 6, 5, 4)

        def copy(dx, dy, src, dst, slot):
            return pltpu.make_async_remote_copy(
                src_ref=src, dst_ref=dst, send_sem=send.at[number, slot],
                recv_sem=recv.at[number, opposite[slot]],
                device_id=(p + dx, q + dy), device_id_type=MESH,
            )

        for dx, dy, src, dst, mine, slot in routes:
            @pl.when(exists(dx, dy))
            def _(dx=dx, dy=dy, src=src, dst=dst, slot=slot):
                copy(dx, dy, src, dst, slot).start()

        def arrive():
            for dx, dy, src, dst, mine, slot in routes:
                @pl.when(exists(dx, dy))
                def _(dx=dx, dy=dy, src=src, mine=mine, slot=slot):
                    pltpu.make_async_remote_copy(
                        src_ref=src, dst_ref=mine, send_sem=send.at[number, slot],
                        recv_sem=recv.at[number, slot],
                        device_id=(p + dx, q + dy), device_id_type=MESH,
                    ).wait_recv()

        def leave():
            for dx, dy, src, dst, mine, slot in routes:
                @pl.when(exists(dx, dy))
                def _(dx=dx, dy=dy, src=src, dst=dst, slot=slot):
                    copy(dx, dy, src, dst, slot).wait_send()

        return arrive, leave

    def to_lines(number, source, target):
        def rows(who):
            return pl.ds(pl.multiple_of(who * cy, cy), cy)

        def copy(other, sender):
            return pltpu.make_async_remote_copy(
                src_ref=source(other), dst_ref=target(sender), send_sem=a2a_send.at[number, other],
                recv_sem=a2a_recv.at[number, sender], device_id=(p, other), device_id_type=MESH,
            )

        def begin(k, _):
            copy(lax.rem(q + k, n_sy), q).start()
            return 0

        def finish(k, _):
            other = lax.rem(q + k, n_sy)
            copy(other, q).wait_send()
            copy(other, other).wait_recv()
            return 0

        lax.fori_loop(1, n_sy, begin, 0)
        own = pltpu.make_async_copy(source(q), target(q), local_sem.at[number])
        own.start()

        def complete():
            lax.fori_loop(1, n_sy, finish, 0)
            own.wait()

        return complete

    def lines(who):
        return pl.ds(pl.multiple_of(who * cy, cy), cy)

    def half_lines(who):
        return pl.ds(pl.multiple_of(who * hy, hy), hy)

    blk_arrive, blk_leave = exchange(
        0, (blk.at[pl.ds(0, H)], blk.at[pl.ds(hx - H, H)]), (blk_y.at[0], blk_y.at[1]),
        [blk_c.at[at] for at in range(4)], got_bx, got_by, got_bc)
    res_arrive, res_leave = exchange(
        1, (right_ref.at[pl.ds(0, M)], right_ref.at[pl.ds(cx - M, M)]), (res_y.at[0], res_y.at[1]),
        [res_c.at[at] for at in range(4)], got_rx, got_ry, got_rc)
    lines_c = to_lines(
        0, lambda s: blk.at[pl.ds((s * m) // 2, mb)], lambda s: line_c.at[:, half_lines(s), :])
    lines_v = to_lines(
        1, lambda s: velocity_ref.at[:, pl.ds(s * m, m)], lambda s: line_v.at[:, :, lines(s), :])

    blk_arrive()
    wide_blk[H : H + hx, H : H + hy, :] = blk[...]
    wide_blk[0:H, H : H + hy, :] = got_bx[0]
    wide_blk[H + hx : hx + 2 * H, H : H + hy, :] = got_bx[1]
    wide_blk[H : H + hx, 0:H, :] = got_by[0]
    wide_blk[H : H + hx, H + hy : hy + 2 * H, :] = got_by[1]
    for at, (dx, dy) in enumerate(DIAGONALS):
        x0, y0 = (0 if dx < 0 else H + hx), (0 if dy < 0 else H + hy)
        wide_blk[x0 : x0 + H, y0 : y0 + H, :] = got_bc[at]
    cond[0] = jnp.zeros((ey, nz), jnp.float32)
    cond[ex // 2 + 1] = jnp.zeros((ey, nz), jnp.float32)
    for j in range(ey // 2):
        cond[1 : ex // 2 + 1, 2 * j : 2 * j + 2, :] = jnp.broadcast_to(
            wide_blk[:, j : j + 1, :], (ex // 2, 2, nz))

    row_at = lax.broadcasted_iota(jnp.int32, (ey, nz), 0)
    lane_at = lax.broadcasted_iota(jnp.int32, (ey, nz), 1)

    def coefficients(pair):
        before, here, after = cond[pair], cond[pair + 1], cond[pair + 2]
        yp = jnp.where(row_at < ey - 1, pltpu.roll(here, ey - 1, 0), 0.0)
        ym = jnp.where(row_at > 0, pltpu.roll(here, 1, 0), 0.0)
        zp = jnp.where(lane_at < nz - 1, pltpu.roll(here, nz - 1, 1), 0.0)
        zm = jnp.where(lane_at > 0, pltpu.roll(here, 1, 1), 0.0)
        ayp, aym = 0.5 * (here + yp), 0.5 * (here + ym)
        azp, azm = (axial_ratio * 0.5) * (here + zp), (axial_ratio * 0.5) * (here + zm)
        across = ayp + aym + azp + azm
        azp = jnp.where(lane_at < nz - 1, azp, 0.0)
        azm = jnp.where(lane_at > 0, azm, 0.0)
        for side, (xp, xm) in enumerate(((here, before), (after, here))):
            x = 2 * pair + side
            axp, axm = 0.5 * (here + xp), 0.5 * (here + xm)
            total = axp + axm + across
            inside = here > 0.0
            over = jnp.where(inside, 1.0 / jnp.where(inside, total, 1.0), 0.0)
            diag[x] = total
            inv[x] = over
            bxp[x] = axp * over
            bxm[x] = axm * over
            byp[x] = ayp * over
            bym[x] = aym * over
            bzp[x] = azp * over
            bzm[x] = azm * over

    for pair in range(ex // 2):
        coefficients(pair)

    def assemble(own, got_x, got_y, got_c):
        region[M : M + cx, M : M + cy, :] = own[...]
        region[0:M, M : M + cy, :] = got_x[0]
        region[M + cx : ex, M : M + cy, :] = got_x[1]
        region[M : M + cx, 0:M, :] = got_y[0]
        region[M : M + cx, M + cy : ey, :] = got_y[1]
        for at, (dx, dy) in enumerate(DIAGONALS):
            x0, y0 = (0 if dx < 0 else M + cx), (0 if dy < 0 else M + cy)
            region[x0 : x0 + M, y0 : y0 + M, :] = got_c[at]

    def beside(x, below, centre, above):
        total = bxp[x] * above + bxm[x] * below
        total = total + byp[x] * pltpu.roll(centre, ey - 1, 0) + bym[x] * pltpu.roll(centre, 1, 0)
        return total + bzp[x] * pltpu.roll(centre, nz - 1, 1) + bzm[x] * pltpu.roll(centre, 1, 1)

    def precondition(target):
        for x in range(ex):
            start[x] = region[x] * inv[x]
        src = start
        for sweep in range(1, SWEEPS):
            dst = target if sweep == SWEEPS - 1 else (buf_a if sweep % 2 else buf_b)

            below, centre = src[sweep - 1], src[sweep]
            for x in range(sweep, ex - sweep):
                above = src[x + 1]
                dst[x] = start[x] + beside(x, below, centre, above)
                below, centre = centre, above
            src = dst

    def send_faces(number, field, packed, got_x, got_y):
        packed[0] = field[M : M + cx, M : M + 1, :]
        packed[1] = field[M : M + cx, M + cy - 1 : M + cy, :]
        return exchange(
            number, (field.at[M], field.at[M + cx - 1]), (packed.at[0], packed.at[1]), None, got_x, got_y, None)

    def place_faces(field, own, got_x, got_y):
        field[M - 1] = got_x[0]
        field[M + cx] = got_x[1]
        field[M : M + cx, M - 1 : M, :] = got_y[0]
        field[M : M + cx, M + cy : M + cy + 1, :] = got_y[1]
        own[...] = field[M - 1 : M + cx + 1, M : M + cy, :]

    def operate(field, x):
        centre = field[x]
        return (diag[x] * (centre - beside(x, field[x - 1], centre, field[x + 1])))[M : M + cy, :]

    res_arrive()
    assemble(right_ref, got_rx, got_ry, got_rc)
    precondition(buf_b)
    face_arrive, face_leave = send_faces(0, buf_b, first_y, got_fx, got_fy)
    face_arrive()
    face_leave()
    place_faces(buf_b, first_own, got_fx, got_fy)

    for x in range(cx):
        image[x] = operate(buf_b, M + x)
    img_y[0] = image[:, 0:M, :]
    img_y[1] = image[:, cy - M : cy, :]
    for at, (dx, dy) in enumerate(DIAGONALS):
        x0, y0 = (0 if dx < 0 else cx - M), (0 if dy < 0 else cy - M)
        img_c[at] = image[x0 : x0 + M, y0 : y0 + M, :]
    img_arrive, img_leave = exchange(
        2, (image.at[pl.ds(0, M)], image.at[pl.ds(cx - M, M)]), (img_y.at[0], img_y.at[1]),
        [img_c.at[at] for at in range(4)], got_ix, got_iy, got_ic)
    lines_f = to_lines(
        2, lambda s: first_own.at[pl.ds(s * m, m + 2)], lambda s: line_f.at[:, lines(s), :])

    img_arrive()
    assemble(image, got_ix, got_iy, got_ic)
    precondition(buf_q)
    q_arrive, q_leave = send_faces(1, buf_q, q_y, got_qx, got_qy)
    q_arrive()
    q_leave()
    place_faces(buf_q, q_own, got_qx, got_qy)
    lines_q = to_lines(
        3, lambda s: q_own.at[pl.ds(s * m, m + 2)], lambda s: line_q.at[:, lines(s), :])

    def products(x, carry):
        ri, ii, wi, ww, rw = carry
        r, i, w = right_ref[x], image[x], operate(buf_q, M + x)
        return ri + r * i, ii + i * i, wi + w * i, ww + w * w, rw + r * w

    zero = jnp.zeros((cy, nz), jnp.float32)
    totals = (zero,) * 5
    for x in range(cx):
        totals = products(x, totals)
    packed = jnp.zeros((8, nz), jnp.float32)
    row8 = lax.broadcasted_iota(jnp.int32, (8, nz), 0)
    for at, total in enumerate(totals):
        packed = jnp.where(row8 == at, jnp.sum(total, axis=0, keepdims=True), packed)
    sums_mine[...] = packed

    def gather(axis_at, count, mine, slots, send, recv, device):
        def copy(other, sender):
            return pltpu.make_async_remote_copy(
                src_ref=mine, dst_ref=slots.at[sender], send_sem=send.at[other],
                recv_sem=recv.at[sender], device_id=device(other), device_id_type=MESH)

        def begin(k, _):
            copy(lax.rem(axis_at + k, count), axis_at).start()
            return 0

        def finish(k, _):
            other = lax.rem(axis_at + k, count)
            copy(other, axis_at).wait_send()
            copy(other, other).wait_recv()
            return 0

        lax.fori_loop(1, count, begin, 0)
        slots[axis_at] = mine[...]

        def complete():
            lax.fori_loop(1, count, finish, 0)
            return jnp.sum(slots[...], axis=0)

        return complete

    row_sums = gather(p, n_sx, sums_mine, sums_x, sx_send, sx_recv, lambda other: (other, q))
    lines_v()
    lines_c()
    lines_f()
    loads[3].wait()
    matrix = matrix_ref[...]
    high = matrix.astype(jnp.bfloat16)
    low = (matrix - high.astype(jnp.float32)).astype(jnp.bfloat16)
    factors = jnp.concatenate([high, high, low], axis=1)

    def diffuse(field):
        coarse = field.astype(jnp.bfloat16)
        fine = (field - coarse.astype(jnp.float32)).astype(jnp.bfloat16)
        return jnp.dot(
            factors, jnp.concatenate([coarse, fine, coarse], axis=0), preferred_element_type=jnp.float32)

    for row in range(m):
        next_ref[2, row] = diffuse(line_v[2, row])
    stores = [pltpu.make_async_copy(next_ref.at[2], next_hbm.at[2], store_sem.at[2])]
    stores[-1].start()
    sums_row[...] = row_sums()
    all_sums = gather(q, n_sy, sums_row, sums_y, sy_send, sy_recv, lambda other: (p, other))
    blk_leave()
    res_leave()
    img_leave()
    scalars = jnp.sum(all_sums(), axis=1, keepdims=True)
    ri, ii, wi, ww, rw = (scalars[at : at + 1, :] for at in range(5))
    alpha = ri / ii
    gamma = wi / ii
    kappa = (gamma * ri - rw) / (ww - gamma * wi)
    of_first = alpha + kappa * gamma

    for x in range(cx):
        potential_ref[x] = of_first * first_own[x + 1] - kappa * q_own[x + 1]
    stores.append(pltpu.make_async_copy(potential_ref, potential_hbm, store_sem.at[0]))
    stores[-1].start()

    lines_q()
    line_at = lax.broadcasted_iota(jnp.int32, (lines_count, nz), 0)
    planes = [of_first * line_f[row] - kappa * line_q[row] for row in range(m + 2)]
    for row in range(m):
        here = planes[row + 1]
        grad_x = 0.5 * (planes[row + 2] - planes[row])
        up = jnp.where(line_at < lines_count - 1, pltpu.roll(here, lines_count - 1, 0), 0.0)
        down = jnp.where(line_at > 0, pltpu.roll(here, 1, 0), 0.0)
        grad_y = 0.5 * (up - down)
        compact = line_c[row // 2]
        c = coupling * jnp.broadcast_to(
            compact[:, None, :], (lines_count // 2, 2, nz)).reshape(lines_count, nz)
        vx, vy = line_v[0, row], line_v[1, row]
        next_ref[0, row] = diffuse(vx + c * (-grad_y - vx))
        next_ref[1, row] = diffuse(vy + c * (grad_x - vy))
        both = pl.ds(0, 2)
        stores.append(pltpu.make_async_copy(
            next_ref.at[both, row], next_hbm.at[both, row], store_sem.at[3 + row]))
        stores[-1].start()
    for store in stores:
        store.wait()


def per_device(n_sx, n_sy, right_side, class_map, conductivity_table, velocity):
    cx, cy, nz = right_side.shape
    m = cx // n_sy
    assert m * n_sy == cx and (m == 1 or m % 2 == 0)
    mb = max(1, m // 2)
    hx, hy = cx // 2, cy // 2
    M, H = MARGIN, MARGIN // 2
    ex, ey = cx + 2 * M, cy + 2 * M
    ny = cy * n_sy
    matrix = jnp.asarray(line_matrix(ny, cy))

    def vmem(*shape):
        return pltpu.VMEM(shape, jnp.float32)

    wide = vmem(ex, ey, nz)
    dma = pltpu.SemaphoreType.DMA
    scratch = [
        vmem(cx, cy, nz), vmem(3, m, ny, nz), dma((3 + m,)),
        vmem(cx, cy, nz), pltpu.VMEM(class_map.shape, jnp.int32),
        pltpu.SMEM(conductivity_table.shape, jnp.float32), vmem(ny, ny), dma((4,)),
        vmem(hx, hy, nz), vmem(2, hx, H, nz), vmem(4, H, H, nz),
        vmem(2, H, hy, nz), vmem(2, hx, H, nz), vmem(4, H, H, nz),
        vmem(ex // 2, ey // 2, nz), vmem(ex // 2 + 2, ey, nz),
        vmem(2, cx, M, nz), vmem(4, M, M, nz),
        vmem(2, M, cy, nz), vmem(2, cx, M, nz), vmem(4, M, M, nz),
        vmem(2, cx, M, nz), vmem(4, M, M, nz),
        vmem(2, M, cy, nz), vmem(2, cx, M, nz), vmem(4, M, M, nz),
        vmem(2, cx, 1, nz), vmem(2, ey, nz), vmem(2, cx, 1, nz),
        vmem(2, cx, 1, nz), vmem(2, ey, nz), vmem(2, cx, 1, nz),
        wide, wide, wide, wide, wide,
        wide, wide, wide, wide, wide, wide, wide, wide,
        vmem(cx + 2, cy, nz), vmem(cx, cy, nz), vmem(cx + 2, cy, nz),
        vmem(3, m, ny, nz), vmem(mb, ny // 2, nz), vmem(m + 2, ny, nz), vmem(m + 2, ny, nz),
        vmem(8, nz), vmem(n_sx, 8, nz), vmem(8, nz), vmem(n_sy, 8, nz),
        dma((3, 8)), dma((3, 8)), dma((2, 8)), dma((2, 8)),
        dma((4, n_sy)), dma((4, n_sy)), dma((4,)),
        dma((n_sx,)), dma((n_sx,)), dma((n_sy,)), dma((n_sy,)),
    ]
    return pl.pallas_call(
        functools.partial(kernel, n_sx, n_sy),
        out_shape=(
            jax.ShapeDtypeStruct((cx, cy, nz), jnp.float32),
            jax.ShapeDtypeStruct((3, m, ny, nz), jnp.float32),
        ),
        in_specs=[pl.BlockSpec(memory_space=pltpu.MemorySpace.HBM)] * 5,
        out_specs=(pl.BlockSpec(memory_space=pltpu.MemorySpace.HBM),) * 2,
        scratch_shapes=scratch,
        compiler_params=pltpu.CompilerParams(
            collective_id=0, has_side_effects=True, vmem_limit_bytes=61 * 2**20),
    )(right_side, class_map, conductivity_table, velocity, matrix)


def solution(mesh):
    return jax.shard_map(
        functools.partial(per_device, mesh.shape["sx"], mesh.shape["sy"]),
        mesh=mesh,
        in_specs=(P("sx", "sy", None), P("sx", "sy", None), P(), P(None, "sx", "sy", None)),
        out_specs=(P("sx", "sy", None), P(None, ("sx", "sy"), None, None)),
        check_vma=False,
    )
```

```python
import functools

import jax
import jax.numpy as jnp
import numpy as np
from jax import lax
from jax.experimental import pallas as pl
from jax.experimental.pallas import tpu as pltpu
from jax.sharding import PartitionSpec as P

MARGIN = 4
SWEEPS = 5
CLASSES = 8

axial_ratio = 0.0625
coupling = 0.25
highest = lax.Precision.HIGHEST
MESH = pl.DeviceIdType.MESH
DIAGONALS = ((-1, -1), (-1, 1), (1, -1), (1, 1))


def line_matrix(lines_count, cells_side):
    positions = np.arange(lines_count, dtype=np.int64) + 1
    phase = (positions[:, None] * positions[None, :]) % (2 * (lines_count + 1))
    sines = np.sqrt(2.0 / (lines_count + 1)) * np.sin(np.pi * phase / (lines_count + 1))
    half = np.sin(0.5 * np.pi * positions / (lines_count + 1))
    stiff = 8.0 * cells_side * cells_side * half * half
    gain = (1.0 - stiff) / (1.0 + stiff)
    return ((sines * gain[None, :]) @ sines).astype(np.float32)


def kernel(
    n_sx, n_sy, right_hbm, class_hbm, table_hbm, velocity_ref, matrix_hbm,
    potential_ref, next_ref,
    right_ref, class_ref, table_ref, matrix_ref, load_sem,
    blk, blk_y, blk_c, got_bx, got_by, got_bc, wide_blk, cond,
    res_y, res_c, got_rx, got_ry, got_rc,
    img_y, img_c, got_ix, got_iy, got_ic,
    first_y, got_fx, got_fy, q_y, got_qx, got_qy,
    region, start, buf_a, buf_b, buf_q,
    bxp, bxm, byp, bym, bzp, bzm, inv, diag,
    first_own, image, q_own,
    line_v, line_c, line_f, line_q, sums_mine, sums_x, sums_row, sums_y,
    halo_send, halo_recv, face_send, face_recv, a2a_send, a2a_recv, local_sem,
    sx_send, sx_recv, sy_send, sy_recv,
    force_f, force_q, edge_mine, edge_got, edge_send, edge_recv,
):
    p, q = lax.axis_index("sx"), lax.axis_index("sy")
    cx, cy, nz = right_ref.shape
    hx, hy = cx // 2, cy // 2
    m = cx // n_sy
    mb = max(1, m // 2)
    ex, ey = cx + 2 * MARGIN, cy + 2 * MARGIN
    M = MARGIN
    H = M // 2
    lines_count = cy * n_sy

    def exists(dx, dy):
        ok = None
        for at, d, n in ((p, dx, n_sx), (q, dy, n_sy)):
            if d:
                this = (at + d >= 0) & (at + d < n)
                ok = this if ok is None else ok & this
        return ok

    loads = [
        pltpu.make_async_copy(src, dst, load_sem.at[at])
        for at, (src, dst) in enumerate((
            (class_hbm, class_ref), (table_hbm, table_ref), (right_hbm, right_ref), (matrix_hbm, matrix_ref)))
    ]
    for load in loads:
        load.start()

    barrier = pltpu.get_barrier_semaphore()

    def greet_y(k, _):
        pl.semaphore_signal(barrier, inc=1, device_id=(p, lax.rem(q + k, n_sy)), device_id_type=MESH)
        return 0

    def greet_x(k, _):
        pl.semaphore_signal(barrier, inc=1, device_id=(lax.rem(p + k, n_sx), q), device_id_type=MESH)
        return 0

    lax.fori_loop(1, n_sy, greet_y, 0)
    lax.fori_loop(1, n_sx, greet_x, 0)
    for dx, dy in DIAGONALS:
        @pl.when(exists(dx, dy))
        def _(dx=dx, dy=dy):
            pl.semaphore_signal(barrier, inc=1, device_id=(p + dx, q + dy), device_id_type=MESH)

    loads[0].wait()
    loads[1].wait()
    classes = class_ref[...].reshape(hx * hy, class_ref.shape[2])
    picked = jnp.zeros(classes.shape, jnp.float32)
    for one in range(CLASSES):
        picked = jnp.where(classes == one, table_ref[one], picked)
    zb = classes.shape[1]
    per = nz // zb
    wide = lax.broadcasted_iota(jnp.int32, (zb, nz), 1) - per * lax.broadcasted_iota(jnp.int32, (zb, nz), 0)
    spread = jnp.where((wide >= 0) & (wide < per), 1.0, 0.0).astype(jnp.float32)
    blk[...] = jnp.dot(picked, spread, precision=highest, preferred_element_type=jnp.float32).reshape(hx, hy, nz)
    blk_y[0] = blk[:, 0:H, :]
    blk_y[1] = blk[:, hy - H : hy, :]
    loads[2].wait()
    res_y[0] = right_ref[:, 0:M, :]
    res_y[1] = right_ref[:, cy - M : cy, :]
    for at, (dx, dy) in enumerate(DIAGONALS):
        bx0, by0 = (0 if dx < 0 else hx - H), (0 if dy < 0 else hy - H)
        rx0, ry0 = (0 if dx < 0 else cx - M), (0 if dy < 0 else cy - M)
        blk_c[at] = blk[bx0 : bx0 + H, by0 : by0 + H, :]
        res_c[at] = right_ref[rx0 : rx0 + M, ry0 : ry0 + M, :]

    for at, (dx, dy) in enumerate(((-1, 0), (1, 0))):
        @pl.when(jnp.logical_not(exists(dx, dy)))
        def _(at=at):
            for ref in (got_bx, got_rx, got_ix, got_fx, got_qx):
                ref[at] = jnp.zeros(ref.shape[1:], jnp.float32)

    for at, (dx, dy) in enumerate(((0, -1), (0, 1))):
        @pl.when(jnp.logical_not(exists(dx, dy)))
        def _(at=at):
            for ref in (got_by, got_ry, got_iy, got_fy, got_qy):
                ref[at] = jnp.zeros(ref.shape[1:], jnp.float32)

    for at, (dx, dy) in enumerate(DIAGONALS):
        @pl.when(jnp.logical_not(exists(dx, dy)))
        def _(at=at):
            for ref in (got_bc, got_rc, got_ic):
                ref[at] = jnp.zeros(ref.shape[1:], jnp.float32)

    diagonal_count = sum(jnp.where(exists(dx, dy), 1, 0) for dx, dy in DIAGONALS)
    pl.semaphore_wait(barrier, n_sy - 1 + n_sx - 1 + diagonal_count)

    def exchange(number, x_parts, y_parts, c_parts, got_x, got_y, got_c):
        routes = []
        for at, (dx, dy) in enumerate(((-1, 0), (1, 0))):
            routes.append((dx, dy, x_parts[at], got_x.at[1 - at], got_x.at[at], at))
        for at, (dx, dy) in enumerate(((0, -1), (0, 1))):
            routes.append((dx, dy, y_parts[at], got_y.at[1 - at], got_y.at[at], 2 + at))
        if got_c is not None:
            for at, (dx, dy) in enumerate(DIAGONALS):
                routes.append((dx, dy, c_parts[at], got_c.at[3 - at], got_c.at[at], 4 + at))
        send, recv = (halo_send, halo_recv) if got_c is not None else (face_send, face_recv)
        opposite = (1, 0, 3, 2, 7, 6, 5, 4)

        def copy(dx, dy, src, dst, slot):
            return pltpu.make_async_remote_copy(
                src_ref=src, dst_ref=dst, send_sem=send.at[number, slot],
                recv_sem=recv.at[number, opposite[slot]],
                device_id=(p + dx, q + dy), device_id_type=MESH,
            )

        for dx, dy, src, dst, mine, slot in routes:
            @pl.when(exists(dx, dy))
            def _(dx=dx, dy=dy, src=src, dst=dst, slot=slot):
                copy(dx, dy, src, dst, slot).start()

        def arrive():
            for dx, dy, src, dst, mine, slot in routes:
                @pl.when(exists(dx, dy))
                def _(dx=dx, dy=dy, src=src, mine=mine, slot=slot):
                    pltpu.make_async_remote_copy(
                        src_ref=src, dst_ref=mine, send_sem=send.at[number, slot],
                        recv_sem=recv.at[number, slot],
                        device_id=(p + dx, q + dy), device_id_type=MESH,
                    ).wait_recv()

        def leave():
            for dx, dy, src, dst, mine, slot in routes:
                @pl.when(exists(dx, dy))
                def _(dx=dx, dy=dy, src=src, dst=dst, slot=slot):
                    copy(dx, dy, src, dst, slot).wait_send()

        return arrive, leave

    def to_lines(number, source, target):
        def rows(who):
            return pl.ds(pl.multiple_of(who * cy, cy), cy)

        def copy(other, sender):
            return pltpu.make_async_remote_copy(
                src_ref=source(other), dst_ref=target(sender), send_sem=a2a_send.at[number, other],
                recv_sem=a2a_recv.at[number, sender], device_id=(p, other), device_id_type=MESH,
            )

        def begin(k, _):
            copy(lax.rem(q + k, n_sy), q).start()
            return 0

        def finish(k, _):
            other = lax.rem(q + k, n_sy)
            copy(other, q).wait_send()
            copy(other, other).wait_recv()
            return 0

        lax.fori_loop(1, n_sy, begin, 0)
        own = pltpu.make_async_copy(source(q), target(q), local_sem.at[number])
        own.start()

        def complete():
            lax.fori_loop(1, n_sy, finish, 0)
            own.wait()

        return complete

    def lines(who):
        return pl.ds(pl.multiple_of(who * cy, cy), cy)

    def half_lines(who):
        return pl.ds(pl.multiple_of(who * hy, hy), hy)

    blk_arrive, blk_leave = exchange(
        0, (blk.at[pl.ds(0, H)], blk.at[pl.ds(hx - H, H)]), (blk_y.at[0], blk_y.at[1]),
        [blk_c.at[at] for at in range(4)], got_bx, got_by, got_bc)
    res_arrive, res_leave = exchange(
        1, (right_ref.at[pl.ds(0, M)], right_ref.at[pl.ds(cx - M, M)]), (res_y.at[0], res_y.at[1]),
        [res_c.at[at] for at in range(4)], got_rx, got_ry, got_rc)
    lines_c = to_lines(
        0, lambda s: blk.at[pl.ds((s * m) // 2, mb)], lambda s: line_c.at[:, half_lines(s), :])
    lines_v = to_lines(
        1, lambda s: velocity_ref.at[:, pl.ds(s * m, m)], lambda s: line_v.at[:, :, lines(s), :])

    blk_arrive()
    wide_blk[H : H + hx, H : H + hy, :] = blk[...]
    wide_blk[0:H, H : H + hy, :] = got_bx[0]
    wide_blk[H + hx : hx + 2 * H, H : H + hy, :] = got_bx[1]
    wide_blk[H : H + hx, 0:H, :] = got_by[0]
    wide_blk[H : H + hx, H + hy : hy + 2 * H, :] = got_by[1]
    for at, (dx, dy) in enumerate(DIAGONALS):
        x0, y0 = (0 if dx < 0 else H + hx), (0 if dy < 0 else H + hy)
        wide_blk[x0 : x0 + H, y0 : y0 + H, :] = got_bc[at]
    cond[0] = jnp.zeros((ey, nz), jnp.float32)
    cond[ex // 2 + 1] = jnp.zeros((ey, nz), jnp.float32)
    for j in range(ey // 2):
        cond[1 : ex // 2 + 1, 2 * j : 2 * j + 2, :] = jnp.broadcast_to(
            wide_blk[:, j : j + 1, :], (ex // 2, 2, nz))

    row_at = lax.broadcasted_iota(jnp.int32, (ey, nz), 0)
    lane_at = lax.broadcasted_iota(jnp.int32, (ey, nz), 1)

    def coefficients(pair):
        before, here, after = cond[pair], cond[pair + 1], cond[pair + 2]
        yp = jnp.where(row_at < ey - 1, pltpu.roll(here, ey - 1, 0), 0.0)
        ym = jnp.where(row_at > 0, pltpu.roll(here, 1, 0), 0.0)
        zp = jnp.where(lane_at < nz - 1, pltpu.roll(here, nz - 1, 1), 0.0)
        zm = jnp.where(lane_at > 0, pltpu.roll(here, 1, 1), 0.0)
        ayp, aym = 0.5 * (here + yp), 0.5 * (here + ym)
        azp, azm = (axial_ratio * 0.5) * (here + zp), (axial_ratio * 0.5) * (here + zm)
        across = ayp + aym + azp + azm
        azp = jnp.where(lane_at < nz - 1, azp, 0.0)
        azm = jnp.where(lane_at > 0, azm, 0.0)
        for side, (xp, xm) in enumerate(((here, before), (after, here))):
            x = 2 * pair + side
            axp, axm = 0.5 * (here + xp), 0.5 * (here + xm)
            total = axp + axm + across
            inside = here > 0.0
            over = jnp.where(inside, 1.0 / jnp.where(inside, total, 1.0), 0.0)
            diag[x] = total
            inv[x] = over
            bxp[x] = axp * over
            bxm[x] = axm * over
            byp[x] = ayp * over
            bym[x] = aym * over
            bzp[x] = azp * over
            bzm[x] = azm * over

    for pair in range(ex // 2):
        coefficients(pair)

    def assemble(own, got_x, got_y, got_c):
        region[M : M + cx, M : M + cy, :] = own[...]
        region[0:M, M : M + cy, :] = got_x[0]
        region[M + cx : ex, M : M + cy, :] = got_x[1]
        region[M : M + cx, 0:M, :] = got_y[0]
        region[M : M + cx, M + cy : ey, :] = got_y[1]
        for at, (dx, dy) in enumerate(DIAGONALS):
            x0, y0 = (0 if dx < 0 else M + cx), (0 if dy < 0 else M + cy)
            region[x0 : x0 + M, y0 : y0 + M, :] = got_c[at]

    def beside(x, below, centre, above):
        total = bxp[x] * above + bxm[x] * below
        total = total + byp[x] * pltpu.roll(centre, ey - 1, 0) + bym[x] * pltpu.roll(centre, 1, 0)
        return total + bzp[x] * pltpu.roll(centre, nz - 1, 1) + bzm[x] * pltpu.roll(centre, 1, 1)

    def precondition(target):
        for x in range(ex):
            start[x] = region[x] * inv[x]
        src = start
        for sweep in range(1, SWEEPS):
            dst = target if sweep == SWEEPS - 1 else (buf_a if sweep % 2 else buf_b)

            below, centre = src[sweep - 1], src[sweep]
            for x in range(sweep, ex - sweep):
                above = src[x + 1]
                dst[x] = start[x] + beside(x, below, centre, above)
                below, centre = centre, above
            src = dst

    def send_faces(number, field, packed, got_x, got_y):
        packed[0] = field[M : M + cx, M : M + 1, :]
        packed[1] = field[M : M + cx, M + cy - 1 : M + cy, :]
        return exchange(
            number, (field.at[M], field.at[M + cx - 1]), (packed.at[0], packed.at[1]), None, got_x, got_y, None)

    def place_faces(field, own, got_x, got_y):
        field[M - 1] = got_x[0]
        field[M + cx] = got_x[1]
        field[M : M + cx, M - 1 : M, :] = got_y[0]
        field[M : M + cx, M + cy : M + cy + 1, :] = got_y[1]
        if own is not None:
            own[...] = field[M - 1 : M + cx + 1, M : M + cy, :]

    def shift_of(rows):
        at = lax.broadcasted_iota(jnp.int32, rows.shape, 0)
        up = jnp.where(at < lines_count - 1, pltpu.roll(rows, lines_count - 1, 0), 0.0)
        return 0.5 * (up - jnp.where(at > 0, pltpu.roll(rows, 1, 0), 0.0))

    def factor(row):
        return coupling * jnp.broadcast_to(
            line_c[row // 2][:, None, :], (lines_count // 2, 2, nz)).reshape(lines_count, nz)

    def forces(planes, target):
        for row in range(m):
            c = factor(row)
            target[0, row] = diffuse(c * -shift_of(planes[row + 1]))
            target[1, row] = diffuse(c * (0.5 * (planes[row + 2] - planes[row])))

    def operate(field, x):
        centre = field[x]
        return (diag[x] * (centre - beside(x, field[x - 1], centre, field[x + 1])))[M : M + cy, :]

    res_arrive()
    assemble(right_ref, got_rx, got_ry, got_rc)
    precondition(buf_b)
    face_arrive, face_leave = send_faces(0, buf_b, first_y, got_fx, got_fy)
    face_arrive()
    face_leave()
    place_faces(buf_b, first_own, got_fx, got_fy)

    for x in range(cx):
        image[x] = operate(buf_b, M + x)
    img_y[0] = image[:, 0:M, :]
    img_y[1] = image[:, cy - M : cy, :]
    for at, (dx, dy) in enumerate(DIAGONALS):
        x0, y0 = (0 if dx < 0 else cx - M), (0 if dy < 0 else cy - M)
        img_c[at] = image[x0 : x0 + M, y0 : y0 + M, :]
    img_arrive, img_leave = exchange(
        2, (image.at[pl.ds(0, M)], image.at[pl.ds(cx - M, M)]), (img_y.at[0], img_y.at[1]),
        [img_c.at[at] for at in range(4)], got_ix, got_iy, got_ic)
    lines_f = to_lines(
        2, lambda s: first_own.at[pl.ds(s * m, m + 2)], lambda s: line_f.at[:, lines(s), :])

    loads[3].wait()
    matrix = matrix_ref[...]
    high = matrix.astype(jnp.bfloat16)
    low = (matrix - high.astype(jnp.float32)).astype(jnp.bfloat16)
    factors = jnp.concatenate([high, high, low], axis=1)

    def diffuse(field):
        coarse = field.astype(jnp.bfloat16)
        fine = (field - coarse.astype(jnp.float32)).astype(jnp.bfloat16)
        return jnp.dot(
            factors, jnp.concatenate([coarse, fine, coarse], axis=0), preferred_element_type=jnp.float32)

    lines_v()
    lines_c()
    for row in range(m):
        c, vx, vy = factor(row), line_v[0, row], line_v[1, row]
        next_ref[0, row] = diffuse(vx - c * vx)
        next_ref[1, row] = diffuse(vy - c * vy)
        next_ref[2, row] = diffuse(line_v[2, row])

    img_arrive()
    assemble(image, got_ix, got_iy, got_ic)
    precondition(buf_q)
    q_arrive, q_leave = send_faces(1, buf_q, q_y, got_qx, got_qy)
    q_own[0] = jnp.zeros((cy, nz), jnp.float32)
    q_own[cx + 1] = jnp.zeros((cy, nz), jnp.float32)
    q_own[1 : cx + 1] = buf_q[M : M + cx, M : M + cy, :]
    lines_q = to_lines(
        3, lambda s: q_own.at[pl.ds(s * m, m + 2)], lambda s: line_q.at[:, lines(s), :])
    lines_f()
    forces([line_f[row] for row in range(m + 2)], force_f)
    q_arrive()
    q_leave()
    place_faces(buf_q, None, got_qx, got_qy)

    edge_mine[0] = got_qx[0, M : M + cy, :]
    edge_mine[1] = got_qx[1, M : M + cy, :]

    def edge_copy(side, target, sender):
        return pltpu.make_async_remote_copy(
            src_ref=edge_mine.at[side], dst_ref=edge_got.at[lines(sender), :],
            send_sem=edge_send.at[side], recv_sem=edge_recv.at[sender],
            device_id=(p, target), device_id_type=MESH)

    ends = (0, n_sy - 1)
    for side, end in enumerate(ends):
        @pl.when(q != end)
        def _(side=side, end=end):
            edge_copy(side, end, q).start()

        @pl.when(q == end)
        def _(side=side):
            edge_got[lines(q), :] = edge_mine[side]

    def edges():
        for side, end in enumerate(ends):
            @pl.when(q != end)
            def _(side=side, end=end):
                edge_copy(side, end, q).wait_send()

            @pl.when(q == end)
            def _(side=side):
                def finish(k, _):
                    other = lax.rem(q + k, n_sy)
                    edge_copy(side, other, other).wait_recv()
                    return 0

                lax.fori_loop(1, n_sy, finish, 0)

        @pl.when((q != 0) & (q != n_sy - 1))
        def _():
            edge_got[...] = jnp.zeros((lines_count, nz), jnp.float32)

    def products(x, carry):
        ri, ii, wi, ww, rw = carry
        r, i, w = right_ref[x], image[x], operate(buf_q, M + x)
        return ri + r * i, ii + i * i, wi + w * i, ww + w * w, rw + r * w

    zero = jnp.zeros((cy, nz), jnp.float32)
    totals = (zero,) * 5
    for x in range(cx):
        totals = products(x, totals)
    packed = jnp.zeros((8, nz), jnp.float32)
    row8 = lax.broadcasted_iota(jnp.int32, (8, nz), 0)
    for at, total in enumerate(totals):
        packed = jnp.where(row8 == at, jnp.sum(total, axis=0, keepdims=True), packed)
    sums_mine[...] = packed

    def gather(axis_at, count, mine, slots, send, recv, device):
        def copy(other, sender):
            return pltpu.make_async_remote_copy(
                src_ref=mine, dst_ref=slots.at[sender], send_sem=send.at[other],
                recv_sem=recv.at[sender], device_id=device(other), device_id_type=MESH)

        def begin(k, _):
            copy(lax.rem(axis_at + k, count), axis_at).start()
            return 0

        def finish(k, _):
            other = lax.rem(axis_at + k, count)
            copy(other, axis_at).wait_send()
            copy(other, other).wait_recv()
            return 0

        lax.fori_loop(1, count, begin, 0)
        slots[axis_at] = mine[...]

        def complete():
            lax.fori_loop(1, count, finish, 0)
            return jnp.sum(slots[...], axis=0)

        return complete

    row_sums = gather(p, n_sx, sums_mine, sums_x, sx_send, sx_recv, lambda other: (other, q))
    sums_row[...] = row_sums()
    all_sums = gather(q, n_sy, sums_row, sums_y, sy_send, sy_recv, lambda other: (p, other))
    blk_leave()
    res_leave()
    img_leave()
    lines_q()
    edges()
    planes = [line_q[row] for row in range(m + 2)]
    planes[0] = jnp.where(q == 0, edge_got[...], planes[0])
    planes[m + 1] = jnp.where(q == n_sy - 1, edge_got[...], planes[m + 1])
    forces(planes, force_q)
    scalars = jnp.sum(all_sums(), axis=1, keepdims=True)
    ri, ii, wi, ww, rw = (scalars[at : at + 1, :] for at in range(5))
    alpha = ri / ii
    gamma = wi / ii
    kappa = (gamma * ri - rw) / (ww - gamma * wi)
    of_first = alpha + kappa * gamma

    for x in range(cx):
        potential_ref[x] = of_first * first_own[x + 1] - kappa * q_own[x + 1]

    for row in range(m):
        for part in range(2):
            next_ref[part, row] += of_first * force_f[part, row] - kappa * force_q[part, row]


def per_device(n_sx, n_sy, right_side, class_map, conductivity_table, velocity):
    cx, cy, nz = right_side.shape
    m = cx // n_sy
    assert m * n_sy == cx and (m == 1 or m % 2 == 0)
    mb = max(1, m // 2)
    hx, hy = cx // 2, cy // 2
    M, H = MARGIN, MARGIN // 2
    ex, ey = cx + 2 * M, cy + 2 * M
    ny = cy * n_sy
    matrix = jnp.asarray(line_matrix(ny, cy))

    def vmem(*shape):
        return pltpu.VMEM(shape, jnp.float32)

    wide = vmem(ex, ey, nz)
    dma = pltpu.SemaphoreType.DMA
    scratch = [
        vmem(cx, cy, nz), pltpu.VMEM(class_map.shape, jnp.int32),
        pltpu.SMEM(conductivity_table.shape, jnp.float32), vmem(ny, ny), dma((4,)),
        vmem(hx, hy, nz), vmem(2, hx, H, nz), vmem(4, H, H, nz),
        vmem(2, H, hy, nz), vmem(2, hx, H, nz), vmem(4, H, H, nz),
        vmem(ex // 2, ey // 2, nz), vmem(ex // 2 + 2, ey, nz),
        vmem(2, cx, M, nz), vmem(4, M, M, nz),
        vmem(2, M, cy, nz), vmem(2, cx, M, nz), vmem(4, M, M, nz),
        vmem(2, cx, M, nz), vmem(4, M, M, nz),
        vmem(2, M, cy, nz), vmem(2, cx, M, nz), vmem(4, M, M, nz),
        vmem(2, cx, 1, nz), vmem(2, ey, nz), vmem(2, cx, 1, nz),
        vmem(2, cx, 1, nz), vmem(2, ey, nz), vmem(2, cx, 1, nz),
        wide, wide, wide, wide, wide,
        wide, wide, wide, wide, wide, wide, wide, wide,
        vmem(cx + 2, cy, nz), vmem(cx, cy, nz), vmem(cx + 2, cy, nz),
        vmem(3, m, ny, nz), vmem(mb, ny // 2, nz), vmem(m + 2, ny, nz), vmem(m + 2, ny, nz),
        vmem(8, nz), vmem(n_sx, 8, nz), vmem(8, nz), vmem(n_sy, 8, nz),
        dma((3, 8)), dma((3, 8)), dma((2, 8)), dma((2, 8)),
        dma((4, n_sy)), dma((4, n_sy)), dma((4,)),
        dma((n_sx,)), dma((n_sx,)), dma((n_sy,)), dma((n_sy,)),
        vmem(2, m, ny, nz), vmem(2, m, ny, nz), vmem(2, cy, nz), vmem(ny, nz), dma((2,)), dma((n_sy,)),
    ]
    return pl.pallas_call(
        functools.partial(kernel, n_sx, n_sy),
        out_shape=(
            pltpu.VMEM((cx, cy, nz), jnp.float32),
            pltpu.VMEM((3, m, ny, nz), jnp.float32),
        ),
        in_specs=[pl.BlockSpec(memory_space=pltpu.MemorySpace.HBM)] * 5,
        out_specs=(pl.BlockSpec(memory_space=pltpu.VMEM),) * 2,
        scratch_shapes=scratch,
        compiler_params=pltpu.CompilerParams(
            collective_id=0, has_side_effects=True, vmem_limit_bytes=61 * 2**20),
    )(right_side, class_map, conductivity_table, velocity, matrix)


def solution(mesh):
    return jax.shard_map(
        functools.partial(per_device, mesh.shape["sx"], mesh.shape["sy"]),
        mesh=mesh,
        in_specs=(P("sx", "sy", None), P("sx", "sy", None), P(), P(None, "sx", "sy", None)),
        out_specs=(P("sx", "sy", None), P(None, ("sx", "sy"), None, None)),
        check_vma=False,
    )
```

```python
import functools

import jax
import jax.numpy as jnp
import numpy as np
from jax import lax
from jax.experimental import pallas as pl
from jax.experimental.pallas import tpu as pltpu
from jax.sharding import PartitionSpec as P

MARGIN = 4
SWEEPS = 5
CLASSES = 8

axial_ratio = 0.0625
coupling = 0.25
highest = lax.Precision.HIGHEST
MESH = pl.DeviceIdType.MESH
DIAGONALS = ((-1, -1), (-1, 1), (1, -1), (1, 1))


def line_matrix(lines_count, cells_side):
    positions = np.arange(lines_count, dtype=np.int64) + 1
    phase = (positions[:, None] * positions[None, :]) % (2 * (lines_count + 1))
    sines = np.sqrt(2.0 / (lines_count + 1)) * np.sin(np.pi * phase / (lines_count + 1))
    half = np.sin(0.5 * np.pi * positions / (lines_count + 1))
    stiff = 8.0 * cells_side * cells_side * half * half
    gain = (1.0 - stiff) / (1.0 + stiff)
    return ((sines * gain[None, :]) @ sines).astype(np.float32)


def kernel(
    n_sx, n_sy, right_hbm, class_hbm, table_hbm, velocity_ref, matrix_hbm,
    potential_ref, next_ref,
    right_ref, class_ref, table_ref, matrix_ref, load_sem,
    blk, blk_y, blk_c, got_bx, got_by, got_bc, wide_blk, cond,
    res_y, res_c, got_rx, got_ry, got_rc,
    img_y, img_c, got_ix, got_iy, got_ic,
    first_y, got_fx, got_fy, q_y, got_qx, got_qy,
    region, start, buf_a, buf_b, buf_q,
    bxp, bxm, byp, bym, bzp, bzm, inv, diag,
    first_own, image, q_own,
    line_v, line_c, line_f, line_q, sums_mine, sums_x, sums_row, sums_y,
    halo_send, halo_recv, face_send, face_recv, a2a_send, a2a_recv, local_sem,
    sx_send, sx_recv, sy_send, sy_recv,
    force_f, force_q, edge_mine, edge_got, edge_send, edge_recv,
):
    p, q = lax.axis_index("sx"), lax.axis_index("sy")
    cx, cy, nz = right_ref.shape
    hx, hy = cx // 2, cy // 2
    m = cx // n_sy
    mb = max(1, m // 2)
    ex, ey = cx + 2 * MARGIN, cy + 2 * MARGIN
    M = MARGIN
    H = M // 2
    lines_count = cy * n_sy

    def exists(dx, dy):
        ok = None
        for at, d, n in ((p, dx, n_sx), (q, dy, n_sy)):
            if d:
                this = (at + d >= 0) & (at + d < n)
                ok = this if ok is None else ok & this
        return ok

    loads = [
        pltpu.make_async_copy(src, dst, load_sem.at[at])
        for at, (src, dst) in enumerate((
            (class_hbm, class_ref), (table_hbm, table_ref), (right_hbm, right_ref), (matrix_hbm, matrix_ref)))
    ]
    for load in loads:
        load.start()

    barrier = pltpu.get_barrier_semaphore()

    def greet_y(k, _):
        pl.semaphore_signal(barrier, inc=1, device_id=(p, lax.rem(q + k, n_sy)), device_id_type=MESH)
        return 0

    def greet_x(k, _):
        pl.semaphore_signal(barrier, inc=1, device_id=(lax.rem(p + k, n_sx), q), device_id_type=MESH)
        return 0

    lax.fori_loop(1, n_sy, greet_y, 0)
    lax.fori_loop(1, n_sx, greet_x, 0)
    for dx, dy in DIAGONALS:
        @pl.when(exists(dx, dy))
        def _(dx=dx, dy=dy):
            pl.semaphore_signal(barrier, inc=1, device_id=(p + dx, q + dy), device_id_type=MESH)

    loads[0].wait()
    loads[1].wait()
    classes = class_ref[...].reshape(hx * hy, class_ref.shape[2])
    picked = jnp.zeros(classes.shape, jnp.float32)
    for one in range(CLASSES):
        picked = jnp.where(classes == one, table_ref[one], picked)
    zb = classes.shape[1]
    per = nz // zb
    wide = lax.broadcasted_iota(jnp.int32, (zb, nz), 1) - per * lax.broadcasted_iota(jnp.int32, (zb, nz), 0)
    spread = jnp.where((wide >= 0) & (wide < per), 1.0, 0.0).astype(jnp.float32)
    blk[...] = jnp.dot(picked, spread, precision=highest, preferred_element_type=jnp.float32).reshape(hx, hy, nz)
    blk_y[0] = blk[:, 0:H, :]
    blk_y[1] = blk[:, hy - H : hy, :]
    loads[2].wait()
    res_y[0] = right_ref[:, 0:M, :]
    res_y[1] = right_ref[:, cy - M : cy, :]
    for at, (dx, dy) in enumerate(DIAGONALS):
        bx0, by0 = (0 if dx < 0 else hx - H), (0 if dy < 0 else hy - H)
        rx0, ry0 = (0 if dx < 0 else cx - M), (0 if dy < 0 else cy - M)
        blk_c[at] = blk[bx0 : bx0 + H, by0 : by0 + H, :]
        res_c[at] = right_ref[rx0 : rx0 + M, ry0 : ry0 + M, :]

    for at, (dx, dy) in enumerate(((-1, 0), (1, 0))):
        @pl.when(jnp.logical_not(exists(dx, dy)))
        def _(at=at):
            for ref in (got_bx, got_rx, got_ix, got_fx, got_qx):
                ref[at] = jnp.zeros(ref.shape[1:], jnp.float32)

    for at, (dx, dy) in enumerate(((0, -1), (0, 1))):
        @pl.when(jnp.logical_not(exists(dx, dy)))
        def _(at=at):
            for ref in (got_by, got_ry, got_iy, got_fy, got_qy):
                ref[at] = jnp.zeros(ref.shape[1:], jnp.float32)

    for at, (dx, dy) in enumerate(DIAGONALS):
        @pl.when(jnp.logical_not(exists(dx, dy)))
        def _(at=at):
            for ref in (got_bc, got_rc, got_ic):
                ref[at] = jnp.zeros(ref.shape[1:], jnp.float32)

    diagonal_count = sum(jnp.where(exists(dx, dy), 1, 0) for dx, dy in DIAGONALS)
    pl.semaphore_wait(barrier, n_sy - 1 + n_sx - 1 + diagonal_count)

    def exchange(number, x_parts, y_parts, c_parts, got_x, got_y, got_c):
        routes = []
        for at, (dx, dy) in enumerate(((-1, 0), (1, 0))):
            routes.append((dx, dy, x_parts[at], got_x.at[1 - at], got_x.at[at], at))
        for at, (dx, dy) in enumerate(((0, -1), (0, 1))):
            routes.append((dx, dy, y_parts[at], got_y.at[1 - at], got_y.at[at], 2 + at))
        if got_c is not None:
            for at, (dx, dy) in enumerate(DIAGONALS):
                routes.append((dx, dy, c_parts[at], got_c.at[3 - at], got_c.at[at], 4 + at))
        send, recv = (halo_send, halo_recv) if got_c is not None else (face_send, face_recv)
        opposite = (1, 0, 3, 2, 7, 6, 5, 4)

        def copy(dx, dy, src, dst, slot):
            return pltpu.make_async_remote_copy(
                src_ref=src, dst_ref=dst, send_sem=send.at[number, slot],
                recv_sem=recv.at[number, opposite[slot]],
                device_id=(p + dx, q + dy), device_id_type=MESH,
            )

        for dx, dy, src, dst, mine, slot in routes:
            @pl.when(exists(dx, dy))
            def _(dx=dx, dy=dy, src=src, dst=dst, slot=slot):
                copy(dx, dy, src, dst, slot).start()

        def arrive():
            for dx, dy, src, dst, mine, slot in routes:
                @pl.when(exists(dx, dy))
                def _(dx=dx, dy=dy, src=src, mine=mine, slot=slot):
                    pltpu.make_async_remote_copy(
                        src_ref=src, dst_ref=mine, send_sem=send.at[number, slot],
                        recv_sem=recv.at[number, slot],
                        device_id=(p + dx, q + dy), device_id_type=MESH,
                    ).wait_recv()

        def leave():
            for dx, dy, src, dst, mine, slot in routes:
                @pl.when(exists(dx, dy))
                def _(dx=dx, dy=dy, src=src, dst=dst, slot=slot):
                    copy(dx, dy, src, dst, slot).wait_send()

        return arrive, leave

    def take(span, sem):
        pltpu.make_async_copy(span, span, sem).wait()

    def to_lines(number, source, target, span):
        def copy(other, sender):
            return pltpu.make_async_remote_copy(
                src_ref=source(other), dst_ref=target(sender), send_sem=a2a_send.at[number],
                recv_sem=a2a_recv.at[number], device_id=(p, other), device_id_type=MESH,
            )

        def begin(k, _):
            copy(lax.rem(q + k, n_sy), q).start()
            return 0

        lax.fori_loop(1, n_sy, begin, 0)
        own = pltpu.make_async_copy(source(q), target(q), local_sem.at[number])
        own.start()

        def complete():
            take(span, a2a_send.at[number])
            take(span, a2a_recv.at[number])
            own.wait()

        return complete

    def lines(who):
        return pl.ds(pl.multiple_of(who * cy, cy), cy)

    def half_lines(who):
        return pl.ds(pl.multiple_of(who * hy, hy), hy)

    blk_arrive, blk_leave = exchange(
        0, (blk.at[pl.ds(0, H)], blk.at[pl.ds(hx - H, H)]), (blk_y.at[0], blk_y.at[1]),
        [blk_c.at[at] for at in range(4)], got_bx, got_by, got_bc)
    res_arrive, res_leave = exchange(
        1, (right_ref.at[pl.ds(0, M)], right_ref.at[pl.ds(cx - M, M)]), (res_y.at[0], res_y.at[1]),
        [res_c.at[at] for at in range(4)], got_rx, got_ry, got_rc)
    lines_c = to_lines(
        0, lambda s: blk.at[pl.ds((s * m) // 2, mb)], lambda s: line_c.at[:, half_lines(s), :],
        line_c.at[:, pl.ds(0, (n_sy - 1) * hy), :])
    lines_v = to_lines(
        1, lambda s: velocity_ref.at[:, pl.ds(s * m, m)], lambda s: line_v.at[:, :, lines(s), :],
        line_v.at[:, :, pl.ds(0, (n_sy - 1) * cy), :])

    blk_arrive()
    wide_blk[H : H + hx, H : H + hy, :] = blk[...]
    wide_blk[0:H, H : H + hy, :] = got_bx[0]
    wide_blk[H + hx : hx + 2 * H, H : H + hy, :] = got_bx[1]
    wide_blk[H : H + hx, 0:H, :] = got_by[0]
    wide_blk[H : H + hx, H + hy : hy + 2 * H, :] = got_by[1]
    for at, (dx, dy) in enumerate(DIAGONALS):
        x0, y0 = (0 if dx < 0 else H + hx), (0 if dy < 0 else H + hy)
        wide_blk[x0 : x0 + H, y0 : y0 + H, :] = got_bc[at]
    cond[0] = jnp.zeros((ey, nz), jnp.float32)
    cond[ex // 2 + 1] = jnp.zeros((ey, nz), jnp.float32)
    for j in range(ey // 2):
        cond[1 : ex // 2 + 1, 2 * j : 2 * j + 2, :] = jnp.broadcast_to(
            wide_blk[:, j : j + 1, :], (ex // 2, 2, nz))

    row_at = lax.broadcasted_iota(jnp.int32, (ey, nz), 0)
    lane_at = lax.broadcasted_iota(jnp.int32, (ey, nz), 1)

    def coefficients(pair):
        before, here, after = cond[pair], cond[pair + 1], cond[pair + 2]
        yp = jnp.where(row_at < ey - 1, pltpu.roll(here, ey - 1, 0), 0.0)
        ym = jnp.where(row_at > 0, pltpu.roll(here, 1, 0), 0.0)
        zp = jnp.where(lane_at < nz - 1, pltpu.roll(here, nz - 1, 1), 0.0)
        zm = jnp.where(lane_at > 0, pltpu.roll(here, 1, 1), 0.0)
        ayp, aym = 0.5 * (here + yp), 0.5 * (here + ym)
        azp, azm = (axial_ratio * 0.5) * (here + zp), (axial_ratio * 0.5) * (here + zm)
        across = ayp + aym + azp + azm
        azp = jnp.where(lane_at < nz - 1, azp, 0.0)
        azm = jnp.where(lane_at > 0, azm, 0.0)
        for side, (xp, xm) in enumerate(((here, before), (after, here))):
            x = 2 * pair + side
            axp, axm = 0.5 * (here + xp), 0.5 * (here + xm)
            total = axp + axm + across
            inside = here > 0.0
            over = jnp.where(inside, 1.0 / jnp.where(inside, total, 1.0), 0.0)
            diag[x] = total
            inv[x] = over
            bxp[x] = axp * over
            bxm[x] = axm * over
            byp[x] = ayp * over
            bym[x] = aym * over
            bzp[x] = azp * over
            bzm[x] = azm * over

    for pair in range(ex // 2):
        coefficients(pair)

    def assemble(own, got_x, got_y, got_c):
        region[M : M + cx, M : M + cy, :] = own[...]
        region[0:M, M : M + cy, :] = got_x[0]
        region[M + cx : ex, M : M + cy, :] = got_x[1]
        region[M : M + cx, 0:M, :] = got_y[0]
        region[M : M + cx, M + cy : ey, :] = got_y[1]
        for at, (dx, dy) in enumerate(DIAGONALS):
            x0, y0 = (0 if dx < 0 else M + cx), (0 if dy < 0 else M + cy)
            region[x0 : x0 + M, y0 : y0 + M, :] = got_c[at]

    def beside(x, below, centre, above):
        total = bxp[x] * above + bxm[x] * below
        total = total + byp[x] * pltpu.roll(centre, ey - 1, 0) + bym[x] * pltpu.roll(centre, 1, 0)
        return total + bzp[x] * pltpu.roll(centre, nz - 1, 1) + bzm[x] * pltpu.roll(centre, 1, 1)

    def precondition(target):
        for x in range(ex):
            start[x] = region[x] * inv[x]
        src = start
        for sweep in range(1, SWEEPS):
            dst = target if sweep == SWEEPS - 1 else (buf_a if sweep % 2 else buf_b)

            below, centre = src[sweep - 1], src[sweep]
            for x in range(sweep, ex - sweep):
                above = src[x + 1]
                dst[x] = start[x] + beside(x, below, centre, above)
                below, centre = centre, above
            src = dst

    def send_faces(number, field, packed, got_x, got_y):
        packed[0] = field[M : M + cx, M : M + 1, :]
        packed[1] = field[M : M + cx, M + cy - 1 : M + cy, :]
        return exchange(
            number, (field.at[M], field.at[M + cx - 1]), (packed.at[0], packed.at[1]), None, got_x, got_y, None)

    def place_faces(field, own, got_x, got_y):
        field[M - 1] = got_x[0]
        field[M + cx] = got_x[1]
        field[M : M + cx, M - 1 : M, :] = got_y[0]
        field[M : M + cx, M + cy : M + cy + 1, :] = got_y[1]
        if own is not None:
            own[...] = field[M - 1 : M + cx + 1, M : M + cy, :]

    def shift_of(rows):
        at = lax.broadcasted_iota(jnp.int32, rows.shape, 0)
        up = jnp.where(at < lines_count - 1, pltpu.roll(rows, lines_count - 1, 0), 0.0)
        return 0.5 * (up - jnp.where(at > 0, pltpu.roll(rows, 1, 0), 0.0))

    def factor(row):
        return coupling * jnp.broadcast_to(
            line_c[row // 2][:, None, :], (lines_count // 2, 2, nz)).reshape(lines_count, nz)

    def forces(planes, target):
        for row in range(m):
            c = factor(row)
            target[0, row] = diffuse(c * -shift_of(planes[row + 1]))
            target[1, row] = diffuse(c * (0.5 * (planes[row + 2] - planes[row])))

    def operate(field, x):
        centre = field[x]
        return (diag[x] * (centre - beside(x, field[x - 1], centre, field[x + 1])))[M : M + cy, :]

    res_arrive()
    assemble(right_ref, got_rx, got_ry, got_rc)
    precondition(buf_b)
    face_arrive, face_leave = send_faces(0, buf_b, first_y, got_fx, got_fy)
    face_arrive()
    face_leave()
    place_faces(buf_b, first_own, got_fx, got_fy)

    for x in range(cx):
        image[x] = operate(buf_b, M + x)
    img_y[0] = image[:, 0:M, :]
    img_y[1] = image[:, cy - M : cy, :]
    for at, (dx, dy) in enumerate(DIAGONALS):
        x0, y0 = (0 if dx < 0 else cx - M), (0 if dy < 0 else cy - M)
        img_c[at] = image[x0 : x0 + M, y0 : y0 + M, :]
    img_arrive, img_leave = exchange(
        2, (image.at[pl.ds(0, M)], image.at[pl.ds(cx - M, M)]), (img_y.at[0], img_y.at[1]),
        [img_c.at[at] for at in range(4)], got_ix, got_iy, got_ic)
    lines_f = to_lines(
        2, lambda s: first_own.at[pl.ds(s * m, m + 2)], lambda s: line_f.at[:, lines(s), :],
        line_f.at[:, pl.ds(0, (n_sy - 1) * cy), :])

    loads[3].wait()
    matrix = matrix_ref[...]
    high = matrix.astype(jnp.bfloat16)
    low = (matrix - high.astype(jnp.float32)).astype(jnp.bfloat16)
    factors = jnp.concatenate([high, high, low], axis=1)

    def diffuse(field):
        coarse = field.astype(jnp.bfloat16)
        fine = (field - coarse.astype(jnp.float32)).astype(jnp.bfloat16)
        return jnp.dot(
            factors, jnp.concatenate([coarse, fine, coarse], axis=0), preferred_element_type=jnp.float32)

    img_arrive()
    assemble(image, got_ix, got_iy, got_ic)
    precondition(buf_q)
    q_arrive, q_leave = send_faces(1, buf_q, q_y, got_qx, got_qy)
    q_own[0] = jnp.zeros((cy, nz), jnp.float32)
    q_own[cx + 1] = jnp.zeros((cy, nz), jnp.float32)
    q_own[1 : cx + 1] = buf_q[M : M + cx, M : M + cy, :]
    lines_q = to_lines(
        3, lambda s: q_own.at[pl.ds(s * m, m + 2)], lambda s: line_q.at[:, lines(s), :],
        line_q.at[:, pl.ds(0, (n_sy - 1) * cy), :])
    lines_v()
    lines_c()
    for row in range(m):
        c, vx, vy = factor(row), line_v[0, row], line_v[1, row]
        next_ref[0, row] = diffuse(vx - c * vx)
        next_ref[1, row] = diffuse(vy - c * vy)
        next_ref[2, row] = diffuse(line_v[2, row])
    q_arrive()
    q_leave()
    place_faces(buf_q, None, got_qx, got_qy)

    edge_mine[0] = got_qx[0, M : M + cy, :]
    edge_mine[1] = got_qx[1, M : M + cy, :]

    def edge_copy(side, target, sender):
        return pltpu.make_async_remote_copy(
            src_ref=edge_mine.at[side], dst_ref=edge_got.at[lines(sender), :],
            send_sem=edge_send.at[side], recv_sem=edge_recv.at[sender],
            device_id=(p, target), device_id_type=MESH)

    ends = (0, n_sy - 1)
    for side, end in enumerate(ends):
        @pl.when(q != end)
        def _(side=side, end=end):
            edge_copy(side, end, q).start()

        @pl.when(q == end)
        def _(side=side):
            edge_got[lines(q), :] = edge_mine[side]

    def edges():
        for side, end in enumerate(ends):
            @pl.when(q != end)
            def _(side=side, end=end):
                edge_copy(side, end, q).wait_send()

            @pl.when(q == end)
            def _(side=side):
                def finish(k, _):
                    other = lax.rem(q + k, n_sy)
                    edge_copy(side, other, other).wait_recv()
                    return 0

                lax.fori_loop(1, n_sy, finish, 0)

        @pl.when((q != 0) & (q != n_sy - 1))
        def _():
            edge_got[...] = jnp.zeros((lines_count, nz), jnp.float32)

    def products(x, carry):
        ri, ii, wi, ww, rw = carry
        r, i, w = right_ref[x], image[x], operate(buf_q, M + x)
        return ri + r * i, ii + i * i, wi + w * i, ww + w * w, rw + r * w

    zero = jnp.zeros((cy, nz), jnp.float32)
    totals = (zero,) * 5
    for x in range(cx):
        totals = products(x, totals)
    packed = jnp.zeros((8, nz), jnp.float32)
    row8 = lax.broadcasted_iota(jnp.int32, (8, nz), 0)
    for at, total in enumerate(totals):
        packed = jnp.where(row8 == at, jnp.sum(total, axis=0, keepdims=True), packed)
    sums_mine[...] = packed

    def gather(axis_at, count, mine, slots, send, recv, device):
        def copy(other, sender):
            return pltpu.make_async_remote_copy(
                src_ref=mine, dst_ref=slots.at[sender], send_sem=send.at[0],
                recv_sem=recv.at[0], device_id=device(other), device_id_type=MESH)

        def begin(k, _):
            copy(lax.rem(axis_at + k, count), axis_at).start()
            return 0

        lax.fori_loop(1, count, begin, 0)
        slots[axis_at] = mine[...]

        def complete():
            span = slots.at[pl.ds(0, count - 1)]
            take(span, send.at[0])
            take(span, recv.at[0])
            return jnp.sum(slots[...], axis=0)

        return complete

    row_sums = gather(p, n_sx, sums_mine, sums_x, sx_send, sx_recv, lambda other: (other, q))
    lines_f()
    forces([line_f[row] for row in range(m + 2)], force_f)
    sums_row[...] = row_sums()
    all_sums = gather(q, n_sy, sums_row, sums_y, sy_send, sy_recv, lambda other: (p, other))
    blk_leave()
    res_leave()
    img_leave()
    lines_q()
    edges()
    planes = [line_q[row] for row in range(m + 2)]
    planes[0] = jnp.where(q == 0, edge_got[...], planes[0])
    planes[m + 1] = jnp.where(q == n_sy - 1, edge_got[...], planes[m + 1])
    forces(planes, force_q)
    scalars = jnp.sum(all_sums(), axis=1, keepdims=True)
    ri, ii, wi, ww, rw = (scalars[at : at + 1, :] for at in range(5))
    alpha = ri / ii
    gamma = wi / ii
    kappa = (gamma * ri - rw) / (ww - gamma * wi)
    of_first = alpha + kappa * gamma

    for x in range(cx):
        potential_ref[x] = of_first * first_own[x + 1] - kappa * q_own[x + 1]

    for row in range(m):
        for part in range(2):
            next_ref[part, row] += of_first * force_f[part, row] - kappa * force_q[part, row]


def per_device(n_sx, n_sy, right_side, class_map, conductivity_table, velocity):
    cx, cy, nz = right_side.shape
    m = cx // n_sy
    assert m * n_sy == cx and (m == 1 or m % 2 == 0)
    mb = max(1, m // 2)
    hx, hy = cx // 2, cy // 2
    M, H = MARGIN, MARGIN // 2
    ex, ey = cx + 2 * M, cy + 2 * M
    ny = cy * n_sy
    matrix = jnp.asarray(line_matrix(ny, cy))

    def vmem(*shape):
        return pltpu.VMEM(shape, jnp.float32)

    wide = vmem(ex, ey, nz)
    dma = pltpu.SemaphoreType.DMA
    scratch = [
        vmem(cx, cy, nz), pltpu.VMEM(class_map.shape, jnp.int32),
        pltpu.SMEM(conductivity_table.shape, jnp.float32), vmem(ny, ny), dma((4,)),
        vmem(hx, hy, nz), vmem(2, hx, H, nz), vmem(4, H, H, nz),
        vmem(2, H, hy, nz), vmem(2, hx, H, nz), vmem(4, H, H, nz),
        vmem(ex // 2, ey // 2, nz), vmem(ex // 2 + 2, ey, nz),
        vmem(2, cx, M, nz), vmem(4, M, M, nz),
        vmem(2, M, cy, nz), vmem(2, cx, M, nz), vmem(4, M, M, nz),
        vmem(2, cx, M, nz), vmem(4, M, M, nz),
        vmem(2, M, cy, nz), vmem(2, cx, M, nz), vmem(4, M, M, nz),
        vmem(2, cx, 1, nz), vmem(2, ey, nz), vmem(2, cx, 1, nz),
        vmem(2, cx, 1, nz), vmem(2, ey, nz), vmem(2, cx, 1, nz),
        wide, wide, wide, wide, wide,
        wide, wide, wide, wide, wide, wide, wide, wide,
        vmem(cx + 2, cy, nz), vmem(cx, cy, nz), vmem(cx + 2, cy, nz),
        vmem(3, m, ny, nz), vmem(mb, ny // 2, nz), vmem(m + 2, ny, nz), vmem(m + 2, ny, nz),
        vmem(8, nz), vmem(n_sx, 8, nz), vmem(8, nz), vmem(n_sy, 8, nz),
        dma((3, 8)), dma((3, 8)), dma((2, 8)), dma((2, 8)),
        dma((4,)), dma((4,)), dma((4,)),
        dma((1,)), dma((1,)), dma((1,)), dma((1,)),
        vmem(2, m, ny, nz), vmem(2, m, ny, nz), vmem(2, cy, nz), vmem(ny, nz), dma((2,)), dma((n_sy,)),
    ]
    return pl.pallas_call(
        functools.partial(kernel, n_sx, n_sy),
        out_shape=(
            pltpu.VMEM((cx, cy, nz), jnp.float32),
            pltpu.VMEM((3, m, ny, nz), jnp.float32),
        ),
        in_specs=[pl.BlockSpec(memory_space=pltpu.MemorySpace.HBM)] * 5,
        out_specs=(pl.BlockSpec(memory_space=pltpu.VMEM),) * 2,
        scratch_shapes=scratch,
        compiler_params=pltpu.CompilerParams(
            collective_id=0, has_side_effects=True, vmem_limit_bytes=61 * 2**20),
    )(right_side, class_map, conductivity_table, velocity, matrix)


def solution(mesh):
    return jax.shard_map(
        functools.partial(per_device, mesh.shape["sx"], mesh.shape["sy"]),
        mesh=mesh,
        in_specs=(P("sx", "sy", None), P("sx", "sy", None), P(), P(None, "sx", "sy", None)),
        out_specs=(P("sx", "sy", None), P(None, ("sx", "sy"), None, None)),
        check_vma=False,
    )
```

```python
import functools

import jax
import jax.numpy as jnp
import numpy as np
from jax import lax
from jax.experimental import pallas as pl
from jax.experimental.pallas import tpu as pltpu
from jax.sharding import PartitionSpec as P

MARGIN = 4
SWEEPS = 5
CLASSES = 8

axial_ratio = 0.0625
coupling = 0.25
highest = lax.Precision.HIGHEST
MESH = pl.DeviceIdType.MESH
DIAGONALS = ((-1, -1), (-1, 1), (1, -1), (1, 1))


def line_matrix(lines_count, cells_side):
    positions = np.arange(lines_count, dtype=np.int64) + 1
    phase = (positions[:, None] * positions[None, :]) % (2 * (lines_count + 1))
    sines = np.sqrt(2.0 / (lines_count + 1)) * np.sin(np.pi * phase / (lines_count + 1))
    half = np.sin(0.5 * np.pi * positions / (lines_count + 1))
    stiff = 8.0 * cells_side * cells_side * half * half
    gain = (1.0 - stiff) / (1.0 + stiff)
    return ((sines * gain[None, :]) @ sines).astype(np.float32)


def kernel(
    n_sx, n_sy, right_hbm, class_hbm, table_hbm, velocity_ref, matrix_hbm,
    potential_ref, next_ref,
    right_ref, class_ref, table_ref, matrix_ref, load_sem,
    blk, blk_y, blk_c, got_bx, got_by, got_bc, wide_blk, cond,
    res_y, res_c, got_rx, got_ry, got_rc,
    img_y, img_c, got_ix, got_iy, got_ic,
    first_y, got_fx, got_fy, q_y, got_qx, got_qy,
    region, start, buf_a, buf_b, buf_q,
    bxp, bxm, byp, bym, bzp, bzm, inv, diag,
    first_own, image, q_own,
    line_v, line_c, line_f, line_q, sums_mine, sums_x, sums_row, sums_y,
    halo_send, halo_recv, face_send, face_recv, a2a_send, a2a_recv, local_sem,
    sx_send, sx_recv, sy_send, sy_recv,
    force_f, force_q, edge_mine, edge_got, edge_send, edge_recv,
):
    p, q = lax.axis_index("sx"), lax.axis_index("sy")
    cx, cy, nz = right_ref.shape
    hx, hy = cx // 2, cy // 2
    m = cx // n_sy
    mb = max(1, m // 2)
    ex, ey = cx + 2 * MARGIN, cy + 2 * MARGIN
    M = MARGIN
    H = M // 2
    lines_count = cy * n_sy

    def exists(dx, dy):
        ok = None
        for at, d, n in ((p, dx, n_sx), (q, dy, n_sy)):
            if d:
                this = (at + d >= 0) & (at + d < n)
                ok = this if ok is None else ok & this
        return ok

    loads = [
        pltpu.make_async_copy(src, dst, load_sem.at[at])
        for at, (src, dst) in enumerate((
            (class_hbm, class_ref), (table_hbm, table_ref), (right_hbm, right_ref), (matrix_hbm, matrix_ref)))
    ]
    for load in loads:
        load.start()

    barrier = pltpu.get_barrier_semaphore()

    def greet_y(k, _):
        pl.semaphore_signal(barrier, inc=1, device_id=(p, lax.rem(q + k, n_sy)), device_id_type=MESH)
        return 0

    def greet_x(k, _):
        pl.semaphore_signal(barrier, inc=1, device_id=(lax.rem(p + k, n_sx), q), device_id_type=MESH)
        return 0

    lax.fori_loop(1, n_sy, greet_y, 0)
    lax.fori_loop(1, n_sx, greet_x, 0)
    for dx, dy in DIAGONALS:
        @pl.when(exists(dx, dy))
        def _(dx=dx, dy=dy):
            pl.semaphore_signal(barrier, inc=1, device_id=(p + dx, q + dy), device_id_type=MESH)

    loads[0].wait()
    loads[1].wait()
    classes = class_ref[...].reshape(hx * hy, class_ref.shape[2])
    picked = jnp.zeros(classes.shape, jnp.float32)
    for one in range(CLASSES):
        picked = jnp.where(classes == one, table_ref[one], picked)
    zb = classes.shape[1]
    per = nz // zb
    wide = lax.broadcasted_iota(jnp.int32, (zb, nz), 1) - per * lax.broadcasted_iota(jnp.int32, (zb, nz), 0)
    spread = jnp.where((wide >= 0) & (wide < per), 1.0, 0.0).astype(jnp.float32)
    blk[...] = jnp.dot(picked, spread, precision=highest, preferred_element_type=jnp.float32).reshape(hx, hy, nz)
    blk_y[0] = blk[:, 0:H, :]
    blk_y[1] = blk[:, hy - H : hy, :]
    loads[2].wait()
    res_y[0] = right_ref[:, 0:M, :]
    res_y[1] = right_ref[:, cy - M : cy, :]
    for at, (dx, dy) in enumerate(DIAGONALS):
        bx0, by0 = (0 if dx < 0 else hx - H), (0 if dy < 0 else hy - H)
        rx0, ry0 = (0 if dx < 0 else cx - M), (0 if dy < 0 else cy - M)
        blk_c[at] = blk[bx0 : bx0 + H, by0 : by0 + H, :]
        res_c[at] = right_ref[rx0 : rx0 + M, ry0 : ry0 + M, :]

    for at, (dx, dy) in enumerate(((-1, 0), (1, 0))):
        @pl.when(jnp.logical_not(exists(dx, dy)))
        def _(at=at):
            for ref in (got_bx, got_rx, got_ix, got_fx, got_qx):
                ref[at] = jnp.zeros(ref.shape[1:], jnp.float32)

    for at, (dx, dy) in enumerate(((0, -1), (0, 1))):
        @pl.when(jnp.logical_not(exists(dx, dy)))
        def _(at=at):
            for ref in (got_by, got_ry, got_iy, got_fy, got_qy):
                ref[at] = jnp.zeros(ref.shape[1:], jnp.float32)

    for at, (dx, dy) in enumerate(DIAGONALS):
        @pl.when(jnp.logical_not(exists(dx, dy)))
        def _(at=at):
            for ref in (got_bc, got_rc, got_ic):
                ref[at] = jnp.zeros(ref.shape[1:], jnp.float32)

    diagonal_count = sum(jnp.where(exists(dx, dy), 1, 0) for dx, dy in DIAGONALS)
    pl.semaphore_wait(barrier, n_sy - 1 + n_sx - 1 + diagonal_count)

    def exchange(number, x_parts, y_parts, c_parts, got_x, got_y, got_c):
        routes = []
        for at, (dx, dy) in enumerate(((-1, 0), (1, 0))):
            routes.append((dx, dy, x_parts[at], got_x.at[1 - at], got_x.at[at], at))
        for at, (dx, dy) in enumerate(((0, -1), (0, 1))):
            routes.append((dx, dy, y_parts[at], got_y.at[1 - at], got_y.at[at], 2 + at))
        if got_c is not None:
            for at, (dx, dy) in enumerate(DIAGONALS):
                routes.append((dx, dy, c_parts[at], got_c.at[3 - at], got_c.at[at], 4 + at))
        send, recv = (halo_send, halo_recv) if got_c is not None else (face_send, face_recv)
        opposite = (1, 0, 3, 2, 7, 6, 5, 4)

        def copy(dx, dy, src, dst, slot):
            return pltpu.make_async_remote_copy(
                src_ref=src, dst_ref=dst, send_sem=send.at[number, slot],
                recv_sem=recv.at[number, opposite[slot]],
                device_id=(p + dx, q + dy), device_id_type=MESH,
            )

        for dx, dy, src, dst, mine, slot in routes:
            @pl.when(exists(dx, dy))
            def _(dx=dx, dy=dy, src=src, dst=dst, slot=slot):
                copy(dx, dy, src, dst, slot).start()

        def arrive():
            for dx, dy, src, dst, mine, slot in routes:
                @pl.when(exists(dx, dy))
                def _(dx=dx, dy=dy, src=src, mine=mine, slot=slot):
                    pltpu.make_async_remote_copy(
                        src_ref=src, dst_ref=mine, send_sem=send.at[number, slot],
                        recv_sem=recv.at[number, slot],
                        device_id=(p + dx, q + dy), device_id_type=MESH,
                    ).wait_recv()

        def leave():
            for dx, dy, src, dst, mine, slot in routes:
                @pl.when(exists(dx, dy))
                def _(dx=dx, dy=dy, src=src, dst=dst, slot=slot):
                    copy(dx, dy, src, dst, slot).wait_send()

        return arrive, leave

    def take(span, sem):
        pltpu.make_async_copy(span, span, sem).wait()

    def to_lines(number, source, target, span):
        def copy(other, sender):
            return pltpu.make_async_remote_copy(
                src_ref=source(other), dst_ref=target(sender), send_sem=a2a_send.at[number],
                recv_sem=a2a_recv.at[number], device_id=(p, other), device_id_type=MESH,
            )

        def begin(k, _):
            copy(lax.rem(q + k, n_sy), q).start()
            return 0

        lax.fori_loop(1, n_sy, begin, 0)
        own = pltpu.make_async_copy(source(q), target(q), local_sem.at[number])
        own.start()

        def complete():
            take(span, a2a_send.at[number])
            take(span, a2a_recv.at[number])
            own.wait()

        return complete

    def lines(who):
        return pl.ds(pl.multiple_of(who * cy, cy), cy)

    def half_lines(who):
        return pl.ds(pl.multiple_of(who * hy, hy), hy)

    blk_arrive, blk_leave = exchange(
        0, (blk.at[pl.ds(0, H)], blk.at[pl.ds(hx - H, H)]), (blk_y.at[0], blk_y.at[1]),
        [blk_c.at[at] for at in range(4)], got_bx, got_by, got_bc)
    res_arrive, res_leave = exchange(
        1, (right_ref.at[pl.ds(0, M)], right_ref.at[pl.ds(cx - M, M)]), (res_y.at[0], res_y.at[1]),
        [res_c.at[at] for at in range(4)], got_rx, got_ry, got_rc)
    lines_c = to_lines(
        0, lambda s: blk.at[pl.ds((s * m) // 2, mb)], lambda s: line_c.at[:, half_lines(s), :],
        line_c.at[:, pl.ds(0, (n_sy - 1) * hy), :])

    blk_arrive()
    wide_blk[H : H + hx, H : H + hy, :] = blk[...]
    wide_blk[0:H, H : H + hy, :] = got_bx[0]
    wide_blk[H + hx : hx + 2 * H, H : H + hy, :] = got_bx[1]
    wide_blk[H : H + hx, 0:H, :] = got_by[0]
    wide_blk[H : H + hx, H + hy : hy + 2 * H, :] = got_by[1]
    for at, (dx, dy) in enumerate(DIAGONALS):
        x0, y0 = (0 if dx < 0 else H + hx), (0 if dy < 0 else H + hy)
        wide_blk[x0 : x0 + H, y0 : y0 + H, :] = got_bc[at]
    cond[0] = jnp.zeros((ey, nz), jnp.float32)
    cond[ex // 2 + 1] = jnp.zeros((ey, nz), jnp.float32)
    for j in range(ey // 2):
        cond[1 : ex // 2 + 1, 2 * j : 2 * j + 2, :] = jnp.broadcast_to(
            wide_blk[:, j : j + 1, :], (ex // 2, 2, nz))

    row_at = lax.broadcasted_iota(jnp.int32, (ey, nz), 0)
    lane_at = lax.broadcasted_iota(jnp.int32, (ey, nz), 1)

    def coefficients(pair):
        before, here, after = cond[pair], cond[pair + 1], cond[pair + 2]
        yp = jnp.where(row_at < ey - 1, pltpu.roll(here, ey - 1, 0), 0.0)
        ym = jnp.where(row_at > 0, pltpu.roll(here, 1, 0), 0.0)
        zp = jnp.where(lane_at < nz - 1, pltpu.roll(here, nz - 1, 1), 0.0)
        zm = jnp.where(lane_at > 0, pltpu.roll(here, 1, 1), 0.0)
        ayp, aym = 0.5 * (here + yp), 0.5 * (here + ym)
        azp, azm = (axial_ratio * 0.5) * (here + zp), (axial_ratio * 0.5) * (here + zm)
        across = ayp + aym + azp + azm
        azp = jnp.where(lane_at < nz - 1, azp, 0.0)
        azm = jnp.where(lane_at > 0, azm, 0.0)
        for side, (xp, xm) in enumerate(((here, before), (after, here))):
            x = 2 * pair + side
            axp, axm = 0.5 * (here + xp), 0.5 * (here + xm)
            total = axp + axm + across
            inside = here > 0.0
            over = jnp.where(inside, 1.0 / jnp.where(inside, total, 1.0), 0.0)
            diag[x] = total
            inv[x] = over
            bxp[x] = axp * over
            bxm[x] = axm * over
            byp[x] = ayp * over
            bym[x] = aym * over
            bzp[x] = azp * over
            bzm[x] = azm * over

    for pair in range(ex // 2):
        coefficients(pair)

    def assemble(own, got_x, got_y, got_c):
        region[M : M + cx, M : M + cy, :] = own[...]
        region[0:M, M : M + cy, :] = got_x[0]
        region[M + cx : ex, M : M + cy, :] = got_x[1]
        region[M : M + cx, 0:M, :] = got_y[0]
        region[M : M + cx, M + cy : ey, :] = got_y[1]
        for at, (dx, dy) in enumerate(DIAGONALS):
            x0, y0 = (0 if dx < 0 else M + cx), (0 if dy < 0 else M + cy)
            region[x0 : x0 + M, y0 : y0 + M, :] = got_c[at]

    def beside(x, below, centre, above):
        total = bxp[x] * above + bxm[x] * below
        total = total + byp[x] * pltpu.roll(centre, ey - 1, 0) + bym[x] * pltpu.roll(centre, 1, 0)
        return total + bzp[x] * pltpu.roll(centre, nz - 1, 1) + bzm[x] * pltpu.roll(centre, 1, 1)

    def precondition(target):
        for x in range(ex):
            start[x] = region[x] * inv[x]
        src = start
        for sweep in range(1, SWEEPS):
            dst = target if sweep == SWEEPS - 1 else (buf_a if sweep % 2 else buf_b)

            below, centre = src[sweep - 1], src[sweep]
            for x in range(sweep, ex - sweep):
                above = src[x + 1]
                dst[x] = start[x] + beside(x, below, centre, above)
                below, centre = centre, above
            src = dst

    def send_faces(number, field, packed, got_x, got_y):
        packed[0] = field[M : M + cx, M : M + 1, :]
        packed[1] = field[M : M + cx, M + cy - 1 : M + cy, :]
        return exchange(
            number, (field.at[M], field.at[M + cx - 1]), (packed.at[0], packed.at[1]), None, got_x, got_y, None)

    def place_faces(field, own, got_x, got_y):
        field[M - 1] = got_x[0]
        field[M + cx] = got_x[1]
        field[M : M + cx, M - 1 : M, :] = got_y[0]
        field[M : M + cx, M + cy : M + cy + 1, :] = got_y[1]
        if own is not None:
            own[...] = field[M - 1 : M + cx + 1, M : M + cy, :]

    def shift_of(rows):
        at = lax.broadcasted_iota(jnp.int32, rows.shape, 0)
        up = jnp.where(at < lines_count - 1, pltpu.roll(rows, lines_count - 1, 0), 0.0)
        return 0.5 * (up - jnp.where(at > 0, pltpu.roll(rows, 1, 0), 0.0))

    def factor(row):
        return coupling * jnp.broadcast_to(
            line_c[row // 2][:, None, :], (lines_count // 2, 2, nz)).reshape(lines_count, nz)

    def forces(planes, target):
        for row in range(m):
            c = factor(row)
            target[0, row] = diffuse(c * -shift_of(planes[row + 1]))
            target[1, row] = diffuse(c * (0.5 * (planes[row + 2] - planes[row])))

    def operate(field, x):
        centre = field[x]
        return (diag[x] * (centre - beside(x, field[x - 1], centre, field[x + 1])))[M : M + cy, :]

    res_arrive()
    assemble(right_ref, got_rx, got_ry, got_rc)
    precondition(buf_b)
    face_arrive, face_leave = send_faces(0, buf_b, first_y, got_fx, got_fy)
    lines_v = to_lines(
        1, lambda s: velocity_ref.at[:, pl.ds(s * m, m)], lambda s: line_v.at[:, :, lines(s), :],
        line_v.at[:, :, pl.ds(0, (n_sy - 1) * cy), :])
    face_arrive()
    face_leave()
    place_faces(buf_b, first_own, got_fx, got_fy)

    for x in range(cx):
        image[x] = operate(buf_b, M + x)
    img_y[0] = image[:, 0:M, :]
    img_y[1] = image[:, cy - M : cy, :]
    for at, (dx, dy) in enumerate(DIAGONALS):
        x0, y0 = (0 if dx < 0 else cx - M), (0 if dy < 0 else cy - M)
        img_c[at] = image[x0 : x0 + M, y0 : y0 + M, :]
    img_arrive, img_leave = exchange(
        2, (image.at[pl.ds(0, M)], image.at[pl.ds(cx - M, M)]), (img_y.at[0], img_y.at[1]),
        [img_c.at[at] for at in range(4)], got_ix, got_iy, got_ic)
    lines_f = to_lines(
        2, lambda s: first_own.at[pl.ds(s * m, m + 2)], lambda s: line_f.at[:, lines(s), :],
        line_f.at[:, pl.ds(0, (n_sy - 1) * cy), :])

    loads[3].wait()
    matrix = matrix_ref[...]
    high = matrix.astype(jnp.bfloat16)
    low = (matrix - high.astype(jnp.float32)).astype(jnp.bfloat16)
    factors = jnp.concatenate([high, high, low], axis=1)

    def diffuse(field):
        coarse = field.astype(jnp.bfloat16)
        fine = (field - coarse.astype(jnp.float32)).astype(jnp.bfloat16)
        return jnp.dot(
            factors, jnp.concatenate([coarse, fine, coarse], axis=0), preferred_element_type=jnp.float32)

    img_arrive()
    assemble(image, got_ix, got_iy, got_ic)
    precondition(buf_q)
    q_arrive, q_leave = send_faces(1, buf_q, q_y, got_qx, got_qy)
    q_own[0] = jnp.zeros((cy, nz), jnp.float32)
    q_own[cx + 1] = jnp.zeros((cy, nz), jnp.float32)
    q_own[1 : cx + 1] = buf_q[M : M + cx, M : M + cy, :]
    lines_q = to_lines(
        3, lambda s: q_own.at[pl.ds(s * m, m + 2)], lambda s: line_q.at[:, lines(s), :],
        line_q.at[:, pl.ds(0, (n_sy - 1) * cy), :])
    lines_v()
    lines_c()
    for row in range(m):
        c, vx, vy = factor(row), line_v[0, row], line_v[1, row]
        next_ref[0, row] = diffuse(vx - c * vx)
        next_ref[1, row] = diffuse(vy - c * vy)
        next_ref[2, row] = diffuse(line_v[2, row])
    q_arrive()
    q_leave()
    place_faces(buf_q, None, got_qx, got_qy)

    edge_mine[0] = got_qx[0, M : M + cy, :]
    edge_mine[1] = got_qx[1, M : M + cy, :]

    def edge_copy(side, target, sender):
        return pltpu.make_async_remote_copy(
            src_ref=edge_mine.at[side], dst_ref=edge_got.at[lines(sender), :],
            send_sem=edge_send.at[side], recv_sem=edge_recv.at[sender],
            device_id=(p, target), device_id_type=MESH)

    ends = (0, n_sy - 1)
    for side, end in enumerate(ends):
        @pl.when(q != end)
        def _(side=side, end=end):
            edge_copy(side, end, q).start()

        @pl.when(q == end)
        def _(side=side):
            edge_got[lines(q), :] = edge_mine[side]

    def edges():
        for side, end in enumerate(ends):
            @pl.when(q != end)
            def _(side=side, end=end):
                edge_copy(side, end, q).wait_send()

            @pl.when(q == end)
            def _(side=side):
                def finish(k, _):
                    other = lax.rem(q + k, n_sy)
                    edge_copy(side, other, other).wait_recv()
                    return 0

                lax.fori_loop(1, n_sy, finish, 0)

        @pl.when((q != 0) & (q != n_sy - 1))
        def _():
            edge_got[...] = jnp.zeros((lines_count, nz), jnp.float32)

    def products(x, carry):
        ri, ii, wi, ww, rw = carry
        r, i, w = right_ref[x], image[x], operate(buf_q, M + x)
        return ri + r * i, ii + i * i, wi + w * i, ww + w * w, rw + r * w

    zero = jnp.zeros((cy, nz), jnp.float32)
    totals = (zero,) * 5
    for x in range(cx):
        totals = products(x, totals)
    packed = jnp.zeros((8, nz), jnp.float32)
    row8 = lax.broadcasted_iota(jnp.int32, (8, nz), 0)
    for at, total in enumerate(totals):
        packed = jnp.where(row8 == at, jnp.sum(total, axis=0, keepdims=True), packed)
    sums_mine[...] = packed

    def gather(axis_at, count, mine, slots, send, recv, device):
        def copy(other, sender):
            return pltpu.make_async_remote_copy(
                src_ref=mine, dst_ref=slots.at[sender], send_sem=send.at[0],
                recv_sem=recv.at[0], device_id=device(other), device_id_type=MESH)

        def begin(k, _):
            copy(lax.rem(axis_at + k, count), axis_at).start()
            return 0

        lax.fori_loop(1, count, begin, 0)
        slots[axis_at] = mine[...]

        def complete():
            span = slots.at[pl.ds(0, count - 1)]
            take(span, send.at[0])
            take(span, recv.at[0])
            return jnp.sum(slots[...], axis=0)

        return complete

    row_sums = gather(p, n_sx, sums_mine, sums_x, sx_send, sx_recv, lambda other: (other, q))
    lines_f()
    forces([line_f[row] for row in range(m + 2)], force_f)
    sums_row[...] = row_sums()
    all_sums = gather(q, n_sy, sums_row, sums_y, sy_send, sy_recv, lambda other: (p, other))
    blk_leave()
    res_leave()
    img_leave()
    lines_q()
    edges()
    planes = [line_q[row] for row in range(m + 2)]
    planes[0] = jnp.where(q == 0, edge_got[...], planes[0])
    planes[m + 1] = jnp.where(q == n_sy - 1, edge_got[...], planes[m + 1])
    forces(planes, force_q)
    scalars = jnp.sum(all_sums(), axis=1, keepdims=True)
    ri, ii, wi, ww, rw = (scalars[at : at + 1, :] for at in range(5))
    alpha = ri / ii
    gamma = wi / ii
    kappa = (gamma * ri - rw) / (ww - gamma * wi)
    of_first = alpha + kappa * gamma

    for x in range(cx):
        potential_ref[x] = of_first * first_own[x + 1] - kappa * q_own[x + 1]

    for row in range(m):
        for part in range(2):
            next_ref[part, row] += of_first * force_f[part, row] - kappa * force_q[part, row]


def per_device(n_sx, n_sy, right_side, class_map, conductivity_table, velocity):
    cx, cy, nz = right_side.shape
    m = cx // n_sy
    assert m * n_sy == cx and (m == 1 or m % 2 == 0)
    mb = max(1, m // 2)
    hx, hy = cx // 2, cy // 2
    M, H = MARGIN, MARGIN // 2
    ex, ey = cx + 2 * M, cy + 2 * M
    ny = cy * n_sy
    matrix = jnp.asarray(line_matrix(ny, cy))

    def vmem(*shape):
        return pltpu.VMEM(shape, jnp.float32)

    wide = vmem(ex, ey, nz)
    dma = pltpu.SemaphoreType.DMA
    scratch = [
        vmem(cx, cy, nz), pltpu.VMEM(class_map.shape, jnp.int32),
        pltpu.SMEM(conductivity_table.shape, jnp.float32), vmem(ny, ny), dma((4,)),
        vmem(hx, hy, nz), vmem(2, hx, H, nz), vmem(4, H, H, nz),
        vmem(2, H, hy, nz), vmem(2, hx, H, nz), vmem(4, H, H, nz),
        vmem(ex // 2, ey // 2, nz), vmem(ex // 2 + 2, ey, nz),
        vmem(2, cx, M, nz), vmem(4, M, M, nz),
        vmem(2, M, cy, nz), vmem(2, cx, M, nz), vmem(4, M, M, nz),
        vmem(2, cx, M, nz), vmem(4, M, M, nz),
        vmem(2, M, cy, nz), vmem(2, cx, M, nz), vmem(4, M, M, nz),
        vmem(2, cx, 1, nz), vmem(2, ey, nz), vmem(2, cx, 1, nz),
        vmem(2, cx, 1, nz), vmem(2, ey, nz), vmem(2, cx, 1, nz),
        wide, wide, wide, wide, wide,
        wide, wide, wide, wide, wide, wide, wide, wide,
        vmem(cx + 2, cy, nz), vmem(cx, cy, nz), vmem(cx + 2, cy, nz),
        vmem(3, m, ny, nz), vmem(mb, ny // 2, nz), vmem(m + 2, ny, nz), vmem(m + 2, ny, nz),
        vmem(8, nz), vmem(n_sx, 8, nz), vmem(8, nz), vmem(n_sy, 8, nz),
        dma((3, 8)), dma((3, 8)), dma((2, 8)), dma((2, 8)),
        dma((4,)), dma((4,)), dma((4,)),
        dma((1,)), dma((1,)), dma((1,)), dma((1,)),
        vmem(2, m, ny, nz), vmem(2, m, ny, nz), vmem(2, cy, nz), vmem(ny, nz), dma((2,)), dma((n_sy,)),
    ]
    return pl.pallas_call(
        functools.partial(kernel, n_sx, n_sy),
        out_shape=(
            pltpu.VMEM((cx, cy, nz), jnp.float32),
            pltpu.VMEM((3, m, ny, nz), jnp.float32),
        ),
        in_specs=[pl.BlockSpec(memory_space=pltpu.MemorySpace.HBM)] * 5,
        out_specs=(pl.BlockSpec(memory_space=pltpu.VMEM),) * 2,
        scratch_shapes=scratch,
        compiler_params=pltpu.CompilerParams(
            collective_id=0, has_side_effects=True, vmem_limit_bytes=61 * 2**20),
    )(right_side, class_map, conductivity_table, velocity, matrix)


def solution(mesh):
    return jax.shard_map(
        functools.partial(per_device, mesh.shape["sx"], mesh.shape["sy"]),
        mesh=mesh,
        in_specs=(P("sx", "sy", None), P("sx", "sy", None), P(), P(None, "sx", "sy", None)),
        out_specs=(P("sx", "sy", None), P(None, ("sx", "sy"), None, None)),
        check_vma=False,
    )
```

```python
import functools

import jax
import jax.numpy as jnp
import numpy as np
from jax import lax
from jax.experimental import pallas as pl
from jax.experimental.pallas import tpu as pltpu
from jax.sharding import PartitionSpec as P

MARGIN = 4
SWEEPS = 5
CLASSES = 8

axial_ratio = 0.0625
coupling = 0.25
highest = lax.Precision.HIGHEST
MESH = pl.DeviceIdType.MESH
DIAGONALS = ((-1, -1), (-1, 1), (1, -1), (1, 1))


def line_matrix(lines_count, cells_side):
    positions = np.arange(lines_count, dtype=np.int64) + 1
    phase = (positions[:, None] * positions[None, :]) % (2 * (lines_count + 1))
    sines = np.sqrt(2.0 / (lines_count + 1)) * np.sin(np.pi * phase / (lines_count + 1))
    half = np.sin(0.5 * np.pi * positions / (lines_count + 1))
    stiff = 8.0 * cells_side * cells_side * half * half
    gain = (1.0 - stiff) / (1.0 + stiff)
    return ((sines * gain[None, :]) @ sines).astype(np.float32)


def kernel(
    n_sx, n_sy, right_hbm, class_hbm, table_hbm, velocity_ref, matrix_hbm,
    potential_ref, next_ref,
    right_ref, class_ref, table_ref, matrix_ref, load_sem,
    blk, blk_y, blk_c, got_bx, got_by, got_bc, wide_blk, cond,
    res_y, res_c, got_rx, got_ry, got_rc,
    img_y, img_c, got_ix, got_iy, got_ic,
    first_y, got_fx, got_fy, q_y, got_qx, got_qy,
    region, start, buf_a, buf_b, buf_q,
    bxp, bxm, byp, bym, bzp, bzm, inv, diag,
    first_own, image, q_own,
    line_v, line_c, line_f, line_q, sums_mine, sums_x, sums_row, sums_y,
    halo_send, halo_recv, face_send, face_recv, a2a_send, a2a_recv, local_sem,
    sx_send, sx_recv, sy_send, sy_recv,
    force_f, force_q, edge_mine, edge_got, edge_send, edge_recv,
):
    p, q = lax.axis_index("sx"), lax.axis_index("sy")
    cx, cy, nz = right_ref.shape
    hx, hy = cx // 2, cy // 2
    m = cx // n_sy
    mb = max(1, m // 2)
    ex, ey = cx + 2 * MARGIN, cy + 2 * MARGIN
    M = MARGIN
    H = M // 2
    lines_count = cy * n_sy

    def exists(dx, dy):
        ok = None
        for at, d, n in ((p, dx, n_sx), (q, dy, n_sy)):
            if d:
                this = (at + d >= 0) & (at + d < n)
                ok = this if ok is None else ok & this
        return ok

    loads = [
        pltpu.make_async_copy(src, dst, load_sem.at[at])
        for at, (src, dst) in enumerate((
            (class_hbm, class_ref), (table_hbm, table_ref), (right_hbm, right_ref), (matrix_hbm, matrix_ref)))
    ]
    for load in loads:
        load.start()

    barrier = pltpu.get_barrier_semaphore()

    def greet_y(k, _):
        pl.semaphore_signal(barrier, inc=1, device_id=(p, lax.rem(q + k, n_sy)), device_id_type=MESH)
        return 0

    def greet_x(k, _):
        pl.semaphore_signal(barrier, inc=1, device_id=(lax.rem(p + k, n_sx), q), device_id_type=MESH)
        return 0

    lax.fori_loop(1, n_sy, greet_y, 0)
    lax.fori_loop(1, n_sx, greet_x, 0)
    for dx, dy in DIAGONALS:
        @pl.when(exists(dx, dy))
        def _(dx=dx, dy=dy):
            pl.semaphore_signal(barrier, inc=1, device_id=(p + dx, q + dy), device_id_type=MESH)

    loads[0].wait()
    loads[1].wait()
    classes = class_ref[...].reshape(hx * hy, class_ref.shape[2])
    picked = jnp.zeros(classes.shape, jnp.float32)
    for one in range(CLASSES):
        picked = jnp.where(classes == one, table_ref[one], picked)
    zb = classes.shape[1]
    per = nz // zb
    wide = lax.broadcasted_iota(jnp.int32, (zb, nz), 1) - per * lax.broadcasted_iota(jnp.int32, (zb, nz), 0)
    spread = jnp.where((wide >= 0) & (wide < per), 1.0, 0.0).astype(jnp.float32)
    blk[...] = jnp.dot(picked, spread, precision=highest, preferred_element_type=jnp.float32).reshape(hx, hy, nz)
    blk_y[0] = blk[:, 0:H, :]
    blk_y[1] = blk[:, hy - H : hy, :]
    loads[2].wait()
    res_y[0] = right_ref[:, 0:M, :]
    res_y[1] = right_ref[:, cy - M : cy, :]
    for at, (dx, dy) in enumerate(DIAGONALS):
        bx0, by0 = (0 if dx < 0 else hx - H), (0 if dy < 0 else hy - H)
        rx0, ry0 = (0 if dx < 0 else cx - M), (0 if dy < 0 else cy - M)
        blk_c[at] = blk[bx0 : bx0 + H, by0 : by0 + H, :]
        res_c[at] = right_ref[rx0 : rx0 + M, ry0 : ry0 + M, :]

    for at, (dx, dy) in enumerate(((-1, 0), (1, 0))):
        @pl.when(jnp.logical_not(exists(dx, dy)))
        def _(at=at):
            for ref in (got_bx, got_rx, got_ix, got_fx, got_qx):
                ref[at] = jnp.zeros(ref.shape[1:], jnp.float32)

    for at, (dx, dy) in enumerate(((0, -1), (0, 1))):
        @pl.when(jnp.logical_not(exists(dx, dy)))
        def _(at=at):
            for ref in (got_by, got_ry, got_iy, got_fy, got_qy):
                ref[at] = jnp.zeros(ref.shape[1:], jnp.float32)

    for at, (dx, dy) in enumerate(DIAGONALS):
        @pl.when(jnp.logical_not(exists(dx, dy)))
        def _(at=at):
            for ref in (got_bc, got_rc, got_ic):
                ref[at] = jnp.zeros(ref.shape[1:], jnp.float32)

    diagonal_count = sum(jnp.where(exists(dx, dy), 1, 0) for dx, dy in DIAGONALS)
    pl.semaphore_wait(barrier, n_sy - 1 + n_sx - 1 + diagonal_count)

    def exchange(number, x_parts, y_parts, c_parts, got_x, got_y, got_c):
        routes = []
        for at, (dx, dy) in enumerate(((-1, 0), (1, 0))):
            routes.append((dx, dy, x_parts[at], got_x.at[1 - at], got_x.at[at], at))
        for at, (dx, dy) in enumerate(((0, -1), (0, 1))):
            routes.append((dx, dy, y_parts[at], got_y.at[1 - at], got_y.at[at], 2 + at))
        if got_c is not None:
            for at, (dx, dy) in enumerate(DIAGONALS):
                routes.append((dx, dy, c_parts[at], got_c.at[3 - at], got_c.at[at], 4 + at))
        send, recv = (halo_send, halo_recv) if got_c is not None else (face_send, face_recv)
        opposite = (1, 0, 3, 2, 7, 6, 5, 4)

        def copy(dx, dy, src, dst, slot):
            return pltpu.make_async_remote_copy(
                src_ref=src, dst_ref=dst, send_sem=send.at[number, slot],
                recv_sem=recv.at[number, opposite[slot]],
                device_id=(p + dx, q + dy), device_id_type=MESH,
            )

        for dx, dy, src, dst, mine, slot in routes:
            @pl.when(exists(dx, dy))
            def _(dx=dx, dy=dy, src=src, dst=dst, slot=slot):
                copy(dx, dy, src, dst, slot).start()

        def arrive():
            for dx, dy, src, dst, mine, slot in routes:
                @pl.when(exists(dx, dy))
                def _(dx=dx, dy=dy, src=src, mine=mine, slot=slot):
                    pltpu.make_async_remote_copy(
                        src_ref=src, dst_ref=mine, send_sem=send.at[number, slot],
                        recv_sem=recv.at[number, slot],
                        device_id=(p + dx, q + dy), device_id_type=MESH,
                    ).wait_recv()

        def leave():
            for dx, dy, src, dst, mine, slot in routes:
                @pl.when(exists(dx, dy))
                def _(dx=dx, dy=dy, src=src, dst=dst, slot=slot):
                    copy(dx, dy, src, dst, slot).wait_send()

        return arrive, leave

    def take(span, sem):
        pltpu.make_async_copy(span, span, sem).wait()

    def to_lines(number, source, target, span):
        def copy(other, sender):
            return pltpu.make_async_remote_copy(
                src_ref=source(other), dst_ref=target(sender), send_sem=a2a_send.at[number],
                recv_sem=a2a_recv.at[number], device_id=(p, other), device_id_type=MESH,
            )

        def begin(k, _):
            copy(lax.rem(q + k, n_sy), q).start()
            return 0

        lax.fori_loop(1, n_sy, begin, 0)
        own = pltpu.make_async_copy(source(q), target(q), local_sem.at[number])
        own.start()

        def complete():
            take(span, a2a_send.at[number])
            take(span, a2a_recv.at[number])
            own.wait()

        return complete

    def lines(who):
        return pl.ds(pl.multiple_of(who * cy, cy), cy)

    def half_lines(who):
        return pl.ds(pl.multiple_of(who * hy, hy), hy)

    blk_arrive, blk_leave = exchange(
        0, (blk.at[pl.ds(0, H)], blk.at[pl.ds(hx - H, H)]), (blk_y.at[0], blk_y.at[1]),
        [blk_c.at[at] for at in range(4)], got_bx, got_by, got_bc)
    res_arrive, res_leave = exchange(
        1, (right_ref.at[pl.ds(0, M)], right_ref.at[pl.ds(cx - M, M)]), (res_y.at[0], res_y.at[1]),
        [res_c.at[at] for at in range(4)], got_rx, got_ry, got_rc)
    lines_c = to_lines(
        0, lambda s: blk.at[pl.ds((s * m) // 2, mb)], lambda s: line_c.at[:, half_lines(s), :],
        line_c.at[:, pl.ds(0, (n_sy - 1) * hy), :])
    lines_v = to_lines(
        1, lambda s: velocity_ref.at[:, pl.ds(s * m, m)], lambda s: line_v.at[:, :, lines(s), :],
        line_v.at[:, :, pl.ds(0, (n_sy - 1) * cy), :])

    blk_arrive()
    wide_blk[H : H + hx, H : H + hy, :] = blk[...]
    wide_blk[0:H, H : H + hy, :] = got_bx[0]
    wide_blk[H + hx : hx + 2 * H, H : H + hy, :] = got_bx[1]
    wide_blk[H : H + hx, 0:H, :] = got_by[0]
    wide_blk[H : H + hx, H + hy : hy + 2 * H, :] = got_by[1]
    for at, (dx, dy) in enumerate(DIAGONALS):
        x0, y0 = (0 if dx < 0 else H + hx), (0 if dy < 0 else H + hy)
        wide_blk[x0 : x0 + H, y0 : y0 + H, :] = got_bc[at]
    cond[0] = jnp.zeros((ey, nz), jnp.float32)
    cond[ex // 2 + 1] = jnp.zeros((ey, nz), jnp.float32)
    for j in range(ey // 2):
        cond[1 : ex // 2 + 1, 2 * j : 2 * j + 2, :] = jnp.broadcast_to(
            wide_blk[:, j : j + 1, :], (ex // 2, 2, nz))

    row_at = lax.broadcasted_iota(jnp.int32, (ey, nz), 0)
    lane_at = lax.broadcasted_iota(jnp.int32, (ey, nz), 1)

    def coefficients(pair):
        before, here, after = cond[pair], cond[pair + 1], cond[pair + 2]
        yp = jnp.where(row_at < ey - 1, pltpu.roll(here, ey - 1, 0), 0.0)
        ym = jnp.where(row_at > 0, pltpu.roll(here, 1, 0), 0.0)
        zp = jnp.where(lane_at < nz - 1, pltpu.roll(here, nz - 1, 1), 0.0)
        zm = jnp.where(lane_at > 0, pltpu.roll(here, 1, 1), 0.0)
        ayp, aym = 0.5 * (here + yp), 0.5 * (here + ym)
        azp, azm = (axial_ratio * 0.5) * (here + zp), (axial_ratio * 0.5) * (here + zm)
        across = ayp + aym + azp + azm
        azp = jnp.where(lane_at < nz - 1, azp, 0.0)
        azm = jnp.where(lane_at > 0, azm, 0.0)
        for side, (xp, xm) in enumerate(((here, before), (after, here))):
            x = 2 * pair + side
            axp, axm = 0.5 * (here + xp), 0.5 * (here + xm)
            total = axp + axm + across
            inside = here > 0.0
            over = jnp.where(inside, 1.0 / jnp.where(inside, total, 1.0), 0.0)
            diag[x] = total
            inv[x] = over
            bxp[x] = axp * over
            bxm[x] = axm * over
            byp[x] = ayp * over
            bym[x] = aym * over
            bzp[x] = azp * over
            bzm[x] = azm * over

    for pair in range(ex // 2):
        coefficients(pair)

    def assemble(own, got_x, got_y, got_c):
        region[M : M + cx, M : M + cy, :] = own[...]
        region[0:M, M : M + cy, :] = got_x[0]
        region[M + cx : ex, M : M + cy, :] = got_x[1]
        region[M : M + cx, 0:M, :] = got_y[0]
        region[M : M + cx, M + cy : ey, :] = got_y[1]
        for at, (dx, dy) in enumerate(DIAGONALS):
            x0, y0 = (0 if dx < 0 else M + cx), (0 if dy < 0 else M + cy)
            region[x0 : x0 + M, y0 : y0 + M, :] = got_c[at]

    def beside(x, below, centre, above):
        total = bxp[x] * above + bxm[x] * below
        total = total + byp[x] * pltpu.roll(centre, ey - 1, 0) + bym[x] * pltpu.roll(centre, 1, 0)
        return total + bzp[x] * pltpu.roll(centre, nz - 1, 1) + bzm[x] * pltpu.roll(centre, 1, 1)

    def precondition(target):
        for x in range(ex):
            start[x] = region[x] * inv[x]
        src = start
        for sweep in range(1, SWEEPS):
            dst = target if sweep == SWEEPS - 1 else (buf_a if sweep % 2 else buf_b)

            below, centre = src[sweep - 1], src[sweep]
            for x in range(sweep, ex - sweep):
                above = src[x + 1]
                dst[x] = start[x] + beside(x, below, centre, above)
                below, centre = centre, above
            src = dst

    def send_faces(number, field, packed, got_x, got_y):
        packed[0] = field[M : M + cx, M : M + 1, :]
        packed[1] = field[M : M + cx, M + cy - 1 : M + cy, :]
        return exchange(
            number, (field.at[M], field.at[M + cx - 1]), (packed.at[0], packed.at[1]), None, got_x, got_y, None)

    def place_faces(field, own, got_x, got_y):
        field[M - 1] = got_x[0]
        field[M + cx] = got_x[1]
        field[M : M + cx, M - 1 : M, :] = got_y[0]
        field[M : M + cx, M + cy : M + cy + 1, :] = got_y[1]
        if own is not None:
            own[...] = field[M - 1 : M + cx + 1, M : M + cy, :]

    def shift_of(rows):
        at = lax.broadcasted_iota(jnp.int32, rows.shape, 0)
        up = jnp.where(at < lines_count - 1, pltpu.roll(rows, lines_count - 1, 0), 0.0)
        return 0.5 * (up - jnp.where(at > 0, pltpu.roll(rows, 1, 0), 0.0))

    def factor(row):
        return coupling * jnp.broadcast_to(
            line_c[row // 2][:, None, :], (lines_count // 2, 2, nz)).reshape(lines_count, nz)

    def forces(planes, target):
        for row in range(m):
            c = factor(row)
            target[0, row] = diffuse(c * -shift_of(planes[row + 1]))
            target[1, row] = diffuse(c * (0.5 * (planes[row + 2] - planes[row])))

    def operate(field, x):
        centre = field[x]
        return (diag[x] * (centre - beside(x, field[x - 1], centre, field[x + 1])))[M : M + cy, :]

    res_arrive()
    assemble(right_ref, got_rx, got_ry, got_rc)
    precondition(buf_b)
    face_arrive, face_leave = send_faces(0, buf_b, first_y, got_fx, got_fy)
    face_arrive()
    face_leave()
    place_faces(buf_b, first_own, got_fx, got_fy)

    for x in range(cx):
        image[x] = operate(buf_b, M + x)
    img_y[0] = image[:, 0:M, :]
    img_y[1] = image[:, cy - M : cy, :]
    for at, (dx, dy) in enumerate(DIAGONALS):
        x0, y0 = (0 if dx < 0 else cx - M), (0 if dy < 0 else cy - M)
        img_c[at] = image[x0 : x0 + M, y0 : y0 + M, :]
    img_arrive, img_leave = exchange(
        2, (image.at[pl.ds(0, M)], image.at[pl.ds(cx - M, M)]), (img_y.at[0], img_y.at[1]),
        [img_c.at[at] for at in range(4)], got_ix, got_iy, got_ic)
    lines_f = to_lines(
        2, lambda s: first_own.at[pl.ds(s * m, m + 2)], lambda s: line_f.at[:, lines(s), :],
        line_f.at[:, pl.ds(0, (n_sy - 1) * cy), :])

    loads[3].wait()
    matrix = matrix_ref[...]
    high = matrix.astype(jnp.bfloat16)
    low = (matrix - high.astype(jnp.float32)).astype(jnp.bfloat16)
    factors = jnp.concatenate([high, high, low], axis=1)

    def diffuse(field):
        coarse = field.astype(jnp.bfloat16)
        fine = (field - coarse.astype(jnp.float32)).astype(jnp.bfloat16)
        return jnp.dot(
            factors, jnp.concatenate([coarse, fine, coarse], axis=0), preferred_element_type=jnp.float32)

    blk_leave()
    res_leave()
    img_arrive()
    assemble(image, got_ix, got_iy, got_ic)
    precondition(buf_q)
    q_arrive, q_leave = send_faces(1, buf_q, q_y, got_qx, got_qy)
    q_own[0] = jnp.zeros((cy, nz), jnp.float32)
    q_own[cx + 1] = jnp.zeros((cy, nz), jnp.float32)
    q_own[1 : cx + 1] = buf_q[M : M + cx, M : M + cy, :]
    lines_q = to_lines(
        3, lambda s: q_own.at[pl.ds(s * m, m + 2)], lambda s: line_q.at[:, lines(s), :],
        line_q.at[:, pl.ds(0, (n_sy - 1) * cy), :])
    lines_v()
    lines_c()
    for row in range(m):
        c, vx, vy = factor(row), line_v[0, row], line_v[1, row]
        next_ref[0, row] = diffuse(vx - c * vx)
        next_ref[1, row] = diffuse(vy - c * vy)
        next_ref[2, row] = diffuse(line_v[2, row])
    img_leave()
    q_arrive()
    q_leave()
    place_faces(buf_q, None, got_qx, got_qy)

    edge_mine[0] = got_qx[0, M : M + cy, :]
    edge_mine[1] = got_qx[1, M : M + cy, :]

    def edge_copy(side, target, sender):
        return pltpu.make_async_remote_copy(
            src_ref=edge_mine.at[side], dst_ref=edge_got.at[lines(sender), :],
            send_sem=edge_send.at[side], recv_sem=edge_recv.at[sender],
            device_id=(p, target), device_id_type=MESH)

    ends = (0, n_sy - 1)
    for side, end in enumerate(ends):
        @pl.when(q != end)
        def _(side=side, end=end):
            edge_copy(side, end, q).start()

        @pl.when(q == end)
        def _(side=side):
            edge_got[lines(q), :] = edge_mine[side]

    def edges():
        for side, end in enumerate(ends):
            @pl.when(q != end)
            def _(side=side, end=end):
                edge_copy(side, end, q).wait_send()

            @pl.when(q == end)
            def _(side=side):
                def finish(k, _):
                    other = lax.rem(q + k, n_sy)
                    edge_copy(side, other, other).wait_recv()
                    return 0

                lax.fori_loop(1, n_sy, finish, 0)

        @pl.when((q != 0) & (q != n_sy - 1))
        def _():
            edge_got[...] = jnp.zeros((lines_count, nz), jnp.float32)

    def products(x, carry):
        ri, ii, wi, ww, rw = carry
        r, i, w = right_ref[x], image[x], operate(buf_q, M + x)
        return ri + r * i, ii + i * i, wi + w * i, ww + w * w, rw + r * w

    zero = jnp.zeros((cy, nz), jnp.float32)
    totals = (zero,) * 5
    for x in range(cx):
        totals = products(x, totals)
    packed = jnp.zeros((8, nz), jnp.float32)
    row8 = lax.broadcasted_iota(jnp.int32, (8, nz), 0)
    for at, total in enumerate(totals):
        packed = jnp.where(row8 == at, jnp.sum(total, axis=0, keepdims=True), packed)
    sums_mine[...] = packed

    def gather(axis_at, count, mine, slots, send, recv, device):
        def copy(other, sender):
            return pltpu.make_async_remote_copy(
                src_ref=mine, dst_ref=slots.at[sender], send_sem=send.at[0],
                recv_sem=recv.at[0], device_id=device(other), device_id_type=MESH)

        def begin(k, _):
            copy(lax.rem(axis_at + k, count), axis_at).start()
            return 0

        lax.fori_loop(1, count, begin, 0)
        slots[axis_at] = mine[...]

        def complete():
            span = slots.at[pl.ds(0, count - 1)]
            take(span, send.at[0])
            take(span, recv.at[0])
            return jnp.sum(slots[...], axis=0)

        return complete

    row_sums = gather(p, n_sx, sums_mine, sums_x, sx_send, sx_recv, lambda other: (other, q))
    lines_f()
    forces([line_f[row] for row in range(m + 2)], force_f)
    sums_row[...] = row_sums()
    all_sums = gather(q, n_sy, sums_row, sums_y, sy_send, sy_recv, lambda other: (p, other))
    lines_q()
    edges()
    planes = [line_q[row] for row in range(m + 2)]
    planes[0] = jnp.where(q == 0, edge_got[...], planes[0])
    planes[m + 1] = jnp.where(q == n_sy - 1, edge_got[...], planes[m + 1])
    forces(planes, force_q)
    scalars = jnp.sum(all_sums(), axis=1, keepdims=True)
    ri, ii, wi, ww, rw = (scalars[at : at + 1, :] for at in range(5))
    alpha = ri / ii
    gamma = wi / ii
    kappa = (gamma * ri - rw) / (ww - gamma * wi)
    of_first = alpha + kappa * gamma

    for x in range(cx):
        potential_ref[x] = of_first * first_own[x + 1] - kappa * q_own[x + 1]

    for row in range(m):
        for part in range(2):
            next_ref[part, row] += of_first * force_f[part, row] - kappa * force_q[part, row]


def per_device(n_sx, n_sy, right_side, class_map, conductivity_table, velocity):
    cx, cy, nz = right_side.shape
    m = cx // n_sy
    assert m * n_sy == cx and (m == 1 or m % 2 == 0)
    mb = max(1, m // 2)
    hx, hy = cx // 2, cy // 2
    M, H = MARGIN, MARGIN // 2
    ex, ey = cx + 2 * M, cy + 2 * M
    ny = cy * n_sy
    matrix = jnp.asarray(line_matrix(ny, cy))

    def vmem(*shape):
        return pltpu.VMEM(shape, jnp.float32)

    wide = vmem(ex, ey, nz)
    dma = pltpu.SemaphoreType.DMA
    scratch = [
        vmem(cx, cy, nz), pltpu.VMEM(class_map.shape, jnp.int32),
        pltpu.SMEM(conductivity_table.shape, jnp.float32), vmem(ny, ny), dma((4,)),
        vmem(hx, hy, nz), vmem(2, hx, H, nz), vmem(4, H, H, nz),
        vmem(2, H, hy, nz), vmem(2, hx, H, nz), vmem(4, H, H, nz),
        vmem(ex // 2, ey // 2, nz), vmem(ex // 2 + 2, ey, nz),
        vmem(2, cx, M, nz), vmem(4, M, M, nz),
        vmem(2, M, cy, nz), vmem(2, cx, M, nz), vmem(4, M, M, nz),
        vmem(2, cx, M, nz), vmem(4, M, M, nz),
        vmem(2, M, cy, nz), vmem(2, cx, M, nz), vmem(4, M, M, nz),
        vmem(2, cx, 1, nz), vmem(2, ey, nz), vmem(2, cx, 1, nz),
        vmem(2, cx, 1, nz), vmem(2, ey, nz), vmem(2, cx, 1, nz),
        wide, wide, wide, wide, wide,
        wide, wide, wide, wide, wide, wide, wide, wide,
        vmem(cx + 2, cy, nz), vmem(cx, cy, nz), vmem(cx + 2, cy, nz),
        vmem(3, m, ny, nz), vmem(mb, ny // 2, nz), vmem(m + 2, ny, nz), vmem(m + 2, ny, nz),
        vmem(8, nz), vmem(n_sx, 8, nz), vmem(8, nz), vmem(n_sy, 8, nz),
        dma((3, 8)), dma((3, 8)), dma((2, 8)), dma((2, 8)),
        dma((4,)), dma((4,)), dma((4,)),
        dma((1,)), dma((1,)), dma((1,)), dma((1,)),
        vmem(2, m, ny, nz), vmem(2, m, ny, nz), vmem(2, cy, nz), vmem(ny, nz), dma((2,)), dma((n_sy,)),
    ]
    return pl.pallas_call(
        functools.partial(kernel, n_sx, n_sy),
        out_shape=(
            pltpu.VMEM((cx, cy, nz), jnp.float32),
            pltpu.VMEM((3, m, ny, nz), jnp.float32),
        ),
        in_specs=[pl.BlockSpec(memory_space=pltpu.MemorySpace.HBM)] * 5,
        out_specs=(pl.BlockSpec(memory_space=pltpu.VMEM),) * 2,
        scratch_shapes=scratch,
        compiler_params=pltpu.CompilerParams(
            collective_id=0, has_side_effects=True, vmem_limit_bytes=61 * 2**20),
    )(right_side, class_map, conductivity_table, velocity, matrix)


def solution(mesh):
    return jax.shard_map(
        functools.partial(per_device, mesh.shape["sx"], mesh.shape["sy"]),
        mesh=mesh,
        in_specs=(P("sx", "sy", None), P("sx", "sy", None), P(), P(None, "sx", "sy", None)),
        out_specs=(P("sx", "sy", None), P(None, ("sx", "sy"), None, None)),
        check_vma=False,
    )
```
